128 devices in a mesh: tm: 2 (over y_hi), lat: 4 (over x), lon: 16 (over y_lo, z, core).
Axes of the slice: x: 4, y: 4 (y_hi: 2, y_lo: 2; y = y_hi * 2 + y_lo), z: 4, core: 2. Of those that a mesh axis runs over, the one named last changes fastest.
Arguments:
- latents: bfloat16 [4, 160, 512, 384], P('tm', 'lat', 'lon'), may hold values from -60 to 60
- conv_weight: bfloat16 [3, 3, 3, 384, 384], replicated, may hold values from -0.0625 to 0.0625
- conv_bias: float32 [384], replicated, may hold values from -4 to 4
- norm_gain: float32 [384], replicated, may hold values from 0.5 to 1.5
- norm_shift: float32 [384], replicated, may hold values from -3 to 3
Outputs:
- decoded: bfloat16 [4, 160, 512, 384], P('tm', 'lat', 'lon')
The draws below stay inside these ranges and needn't reach their ends.
All inputs are finite; a program needn't handle non-finite values.
Results may differ from the reference program's by a relative error of at most 0.00065.
Values may be sent and summed in bfloat16 or wider, within the bound.
A program may use at most 192 MiB of HBM per device.

```python
import math
import jax
import jax.numpy as jnp
from jax import lax

C = 384
GROUPS = 32
FRAMES = 4
HEIGHT = 160
WIDTH = 512


def draw_latents(key, part):
    key = jax.random.fold_in(key, 17)
    key_noise, key_rough, key_offset = jax.random.split(key, 3)
    time_pos = jnp.arange(FRAMES, dtype=jnp.float32) / max(FRAMES - 1, 1)
    lat_pos = jnp.arange(HEIGHT, dtype=jnp.float32) / max(HEIGHT - 1, 1)
    lon_pos = jnp.arange(WIDTH, dtype=jnp.float32) / max(WIDTH - 1, 1)
    noise_part = jnp.clip(jax.random.normal(key_noise, (FRAMES, HEIGHT, WIDTH, C), jnp.float32), -5.0, 5.0)
    offset = jax.random.uniform(key_offset, (C,), jnp.float32, 0.0, 1.5)
    roughness = jnp.exp(jax.random.uniform(key_rough, (FRAMES, HEIGHT, WIDTH, 1), jnp.float32) * math.log(4.0))
    exponent = lon_pos[None, None, :] + 0.5 * lat_pos[None, :, None] + 0.5 * time_pos[:, None, None]
    trend_scale = jnp.exp(exponent * math.log(3.0))[..., None]
    return (0.3 * trend_scale * (roughness * noise_part + offset)).astype(jnp.bfloat16)


def centred(own_key, dims, deviation, reach, held_as=jnp.bfloat16):
    result = deviation * jax.random.normal(own_key, dims, jnp.float32)
    return jnp.clip(result, min=-reach, max=reach).astype(held_as)


def setup_inputs(seed: int = 0) -> dict:
    key_list = jax.random.split(jax.random.key(seed), 6)
    return {
        "latents": draw_latents(jax.random.fold_in(key_list[5], 71), 0),
        "conv_weight": centred(key_list[1], (3, 3, 3, C, C), (27 * C) ** -0.5, 0.0625),
        "conv_bias": centred(key_list[2], (C,), 1.0, 4.0, jnp.float32),
        "norm_gain": jnp.clip(1.0 + 0.1 * jax.random.normal(key_list[3], (C,), jnp.float32), 0.5, 1.5),
        "norm_shift": centred(key_list[4], (C,), 0.5, 3.0, jnp.float32),
    }


def reference(latents, conv_weight, conv_bias, norm_gain, norm_shift):
    padded = jnp.pad(latents.astype(jnp.float32), ((2, 0), (1, 1), (0, 0), (0, 0)))
    padded = jnp.concatenate([padded[:, :, WIDTH - 1:], padded, padded[:, :, :1]], axis=2)
    weights = conv_weight.astype(jnp.float32)

    def one_frame(frame_idx):
        window = lax.dynamic_slice_in_dim(padded, frame_idx, 3, 0)
        summed = jnp.zeros((HEIGHT * WIDTH, C), jnp.float32)
        for depth_a in range(3):
            for row_b in range(3):
                for col_k in range(3):
                    piece_in = window[depth_a, row_b:row_b + HEIGHT, col_k:col_k + WIDTH, :].reshape(HEIGHT * WIDTH, C)
                    summed = summed + jnp.dot(piece_in, weights[depth_a, row_b, col_k], precision=lax.Precision.HIGHEST, preferred_element_type=jnp.float32)
        return (summed + conv_bias[None, :]).reshape(HEIGHT, WIDTH, C)
    conv_out = lax.map(one_frame, jnp.arange(FRAMES, dtype=jnp.int32))
    grouped = conv_out.reshape(FRAMES, HEIGHT, WIDTH, GROUPS, C // GROUPS)
    group_mean = lax.optimization_barrier(jnp.mean(grouped, axis=(0, 1, 2, 4)))
    centered = grouped - group_mean[None, None, None, :, None]
    group_var = lax.optimization_barrier(jnp.mean(centered * centered, axis=(0, 1, 2, 4)))
    scaled = centered * lax.rsqrt(group_var + 1e-06)[None, None, None, :, None]
    normed = scaled.reshape(FRAMES, HEIGHT, WIDTH, C) * norm_gain + norm_shift
    return jax.nn.silu(normed).astype(jnp.bfloat16)
```

```python
import functools

import jax
import jax.numpy as jnp
from jax import lax
from jax.experimental import pallas as pl
from jax.experimental.pallas import tpu as pltpu
from jax.sharding import PartitionSpec as P

MESH = pl.DeviceIdType.MESH
F32, BF16 = jnp.float32, jnp.bfloat16
HIGH = lax.Precision.HIGHEST

GROUPS = 32
C = 384
PER = C // GROUPS
H, WD = 40, 32
N = 4
CHUNKS = H // N
EDGE = 16

SHARE_LO, SHARE_HI = 15, 29
BACK = (SHARE_HI - SHARE_LO + 2) // N
BACK_ROW = SHARE_LO - 1
OFF = 30
ACC_ROWS = 62


def chunk_row(c):
    odd = c % 2
    half = c // 2
    return N * ((1 - odd) * half + odd * (CHUNKS - 1 - half))


def kernel(
    x_ref, w_ref, bias_ref, gain_ref, shift_ref, o_ref,
    wt, xm, xl, xr, lh, rh, acc, out, g_in, g_out, aff, stat, r1, r2,
    loc_sem, w_sem, out_sem, main_s, main_r, strip_s, strip_r, row_s, row_r, r1_s, r1_r, r2_s, r2_r,
):
    tm, lat, lon = (lax.axis_index(a) for a in ("tm", "lat", "lon"))
    left, right = (lon + 15) % 16, (lon + 1) % 16
    z, yl = lon % 8, lon // 8
    first, second = tm == 0, tm == 1
    has_up, has_dn = lat > 0, lat < 3
    partner = (1 - tm, lat, lon)
    near = [(tm, lat, yl * 8 + (z + d) % 8) for d in range(1, 8)]
    far = [
        ((tm + a) % 2, (lat + b) % 4, ((yl + c) % 2) * 8 + z)
        for a in range(2) for b in range(4) for c in range(2)
    ][1:]
    corners = [(tm, (lat + b) % 4, l) for b in (0, 1, 3) for l in (left, right)]

    barrier = pltpu.get_barrier_semaphore()
    peers = far + near + corners
    for peer in peers:
        pl.semaphore_signal(barrier, inc=1, device_id=peer, device_id_type=MESH)

    def load_x(c):
        return pltpu.make_async_copy(
            x_ref.at[:, pl.ds(c * N, N)], xm.at[pl.ds(2, 2), pl.ds(c * N + 1, N)], loc_sem.at[c])

    def load_w(a):
        return pltpu.make_async_copy(w_ref.at[a], wt.at[a], w_sem.at[a])

    load_x(0).start()
    load_w(2).start()
    load_w(1).start()
    for c in range(1, CHUNKS):
        load_x(c).start()
    load_w(0).start()

    row_i = lax.broadcasted_iota(jnp.int32, (C, 128), 0)
    lane_i = lax.broadcasted_iota(jnp.int32, (C, 128), 1)
    delta = row_i - PER * lane_i
    g_in[...] = jnp.where((delta >= 0) & (delta < PER), 1.0, 0.0)
    row_i = lax.broadcasted_iota(jnp.int32, (128, C), 0)
    lane_i = lax.broadcasted_iota(jnp.int32, (128, C), 1)
    delta = lane_i - PER * row_i
    g_out[...] = jnp.where((delta >= 0) & (delta < PER), 1.0, 0.0)

    pl.semaphore_wait(barrier, len(peers))

    def remote(src, dst, s, r, dev):
        return pltpu.make_async_remote_copy(
            src_ref=src, dst_ref=dst, send_sem=s, recv_sem=r, device_id=dev, device_id_type=MESH)

    def main(c, row):
        return remote(
            x_ref.at[:, pl.ds(row, N)], xm.at[pl.ds(0, 2), pl.ds(row + 1, N)],
            main_s.at[c], main_r.at[c], partner)

    def strip(k, c, p, side):
        cols = pl.ds(WD - EDGE, EDGE) if side == 0 else pl.ds(0, EDGE)
        src = (
            x_ref.at[:, pl.ds(p - 1, N), cols] if k else xm.at[pl.ds(0, 2), pl.ds(p, N), cols])
        dst = (lh, rh)[side].at[pl.ds(2 * k, 2), pl.ds(p, N)]
        return remote(src, dst, strip_s.at[k, c, side], strip_r.at[k, c, side],
                      (tm, lat, (right, left)[side]))

    def rows(k, way):
        p = H if way == 0 else 1
        q = 0 if way == 0 else H + 1
        la = (lat + 1) % 4 if way == 0 else (lat + 3) % 4
        base = x_ref.at[:, pl.ds(p - 1, 1)] if k else xm.at[pl.ds(0, 2), pl.ds(p, 1)]
        to = (pl.ds(2 * k, 2), pl.ds(q, 1))
        ss, rs = row_s.at[k, way], row_r.at[k, way]
        return [
            remote(base, xm.at[to], ss.at[0], rs.at[0], (tm, la, lon)),
            remote(base.at[:, :, pl.ds(WD - EDGE, EDGE)], lh.at[to], ss.at[1], rs.at[1], (tm, la, right)),
            remote(base.at[:, :, pl.ds(0, EDGE)], rh.at[to], ss.at[2], rs.at[2], (tm, la, left)),
        ]

    def rows_start(k, way):
        @pl.when(has_dn if way == 0 else has_up)
        def _():
            for cp in rows(k, way):
                cp.start()

    for way in (0, 1):
        rows_start(1, way)
    for c in range(2):
        for side in (0, 1):
            strip(1, c, c * N + 1, side).start()

    @pl.when(first)
    def _():
        for c in range(CHUNKS):
            main(c, chunk_row(c)).start()

    @pl.when(second)
    def _():
        for c in range(BACK):
            main(c, BACK_ROW + c * N).start()

    for c in range(2, CHUNKS):
        for side in (0, 1):
            strip(1, c, c * N + 1, side).start()

    bias = jnp.broadcast_to(bias_ref[...][None], (2, WD, C))

    def fill(r, carry):
        acc[:, r] = bias
        return carry

    lax.fori_loop(0, ACC_ROWS, fill, 0)

    def shifted(slot, p):
        col = lax.broadcasted_iota(jnp.int32, (WD, C), 0)
        for f in range(2):
            v = xm[slot + f, p].astype(F32)
            a = lh[slot + f, p].astype(F32)[EDGE - 1:]
            b = rh[slot + f, p].astype(F32)[:1]
            xl[slot + f, p] = jnp.where(col == 0, a, pltpu.roll(v, 1, 0)).astype(BF16)
            xr[slot + f, p] = jnp.where(col == WD - 1, b, pltpu.roll(v, WD - 1, 0)).astype(BF16)

    def planes(slot, p, n, own, off, taps=(0, 1, 2)):
        m = n * WD
        both = jnp.concatenate(
            [v[pl.ds(slot, 2), pl.ds(p, n)].reshape(2 * m, C) for v in (xl, xm, xr)], axis=1)
        one = both[:m] if own else both[m:]
        same, target = (2, 1) if own else (0, 0)
        for b in taps:
            rr = pl.ds(p + 1 - b + off, n)
            y = jnp.dot(both, wt[same, b], preferred_element_type=F32)
            acc[:, rr] += y.reshape(2, n, WD, C)
            y = jnp.dot(one, wt[1, b], preferred_element_type=F32)
            acc[target, rr] += y.reshape(n, WD, C)

    def edges(k):
        for way in (0, 1):
            @pl.when(has_up if way == 0 else has_dn)
            def _():
                for cp in rows(k, way):
                    cp.wait_recv()
                p = 0 if way == 0 else H + 1
                shifted(2 * k, p)
                planes(2 * k, p, 1, k == 1, 0, (0,) if way == 0 else (2,))

    def other_p(c):
        return jnp.where(first, BACK_ROW + 1 + c * N, chunk_row(c) + 1)

    def arrive(c):
        p = other_p(c)
        main(c, p - 1).wait_recv()
        for side in (0, 1):
            strip(0, c, p, side).start()

        @pl.when(second & (c == 0))
        def _():
            rows_start(0, 1)

        @pl.when(second & (c == 1))
        def _():
            rows_start(0, 0)

    load_w(2).wait()
    load_w(1).wait()

    def own_step(i, carry):
        mine = i < CHUNKS
        j = jnp.maximum(i - CHUNKS, 0)
        slot = jnp.where(mine, 2, 0)
        p = jnp.where(mine, 1 + i * N, BACK_ROW + 1 + j * N)

        @pl.when(mine)
        def _():
            load_x(i).wait()
            for side in (0, 1):
                strip(1, i, p, side).wait_recv()

        @pl.when(first & (i >= CHUNKS - 1) & (i < CHUNKS - 1 + BACK))
        def _():
            arrive(i - (CHUNKS - 1))

        @pl.when(i >= CHUNKS)
        def _():
            for side in (0, 1):
                strip(0, j, p, side).wait_recv()

        for r in range(N):
            shifted(slot, p + r)
        planes(slot, p, N, True, jnp.where(mine, 0, OFF))
        return carry

    lax.fori_loop(0, jnp.where(first, CHUNKS + BACK, CHUNKS), own_step, 0)
    edges(1)
    load_w(0).wait()

    count = jnp.where(first, 54.0, 26.0) * (2 * WD * PER)
    other_count = jnp.where(first, 26.0, 54.0) * (2 * WD * PER)
    sub = lax.broadcasted_iota(jnp.int32, (8, 128), 0)

    def pack(mean, m2):
        return jnp.where(sub == 0, mean, jnp.where(sub == 1, m2, 0.0))

    def over_rows(f):
        def step(r, a):
            return a + f(acc[:, r].reshape(2 * WD // 8, 8, C)).sum(0)
        a = lax.fori_loop(1, jnp.where(first, 41, 1 + SHARE_LO), step, jnp.zeros((8, C), F32))
        a = lax.fori_loop(
            jnp.where(first, 1 + SHARE_LO + OFF, 1 + SHARE_HI), jnp.where(first, 1 + SHARE_HI + OFF, 41), step, a)
        return jnp.broadcast_to(a.sum(0, keepdims=True), (8, C))

    def group(v):
        return jnp.dot(v, g_in[...], precision=HIGH, preferred_element_type=F32)

    def channel(v):
        return jnp.dot(v, g_out[...], precision=HIGH, preferred_element_type=F32)

    def r1_copy(i):
        return remote(r1.at[0], r1.at[i + 1], r1_s.at[i], r1_r.at[i], near[i])

    def r2_copy(i):
        return remote(r2.at[0], r2.at[i + 1], r2_s.at[i], r2_r.at[i], far[i])

    def stats_begin():
        mean = group(over_rows(lambda v: v)) / count
        mean_c = channel(mean)
        m2 = group(over_rows(lambda v: (v - mean_c) * (v - mean_c)))
        r1[0] = pack(mean, m2)
        for i in range(7):
            r1_copy(i).start()

    def stats_middle():
        for i in range(7):
            r1_copy(i).wait_recv()
        means = [r1[i, 0:1] for i in range(8)]
        mean = sum(means) * 0.125
        m2 = sum(r1[i, 1:2] for i in range(8)) + count * sum((m - mean) * (m - mean) for m in means)
        r2[0] = pack(jnp.broadcast_to(mean, (8, 128)), jnp.broadcast_to(m2, (8, 128)))
        for i in range(15):
            r2_copy(i).start()

    def stats_end():
        for i in range(15):
            r2_copy(i).wait_recv()
        means = [r2[i, 0:1] for i in range(16)]
        mine, other = 8.0 * count, 8.0 * other_count
        total = 8.0 * (mine + other)
        mean = (mine * sum(means[:8]) + other * sum(means[8:])) / total
        m2 = sum(r2[i, 1:2] for i in range(16))
        m2 = m2 + mine * sum((m - mean) * (m - mean) for m in means[:8])
        m2 = m2 + other * sum((m - mean) * (m - mean) for m in means[8:])
        inv = lax.rsqrt(m2 / total + 1e-6)
        both = channel(pack(jnp.broadcast_to(mean, (8, 128)), jnp.broadcast_to(inv, (8, 128))))
        aff[0:1] = both[0:1]
        aff[1:2] = both[1:2] * gain_ref[...]

    def finish(lo, hi):
        mean, scale, shift = aff[0:1], aff[1:2], shift_ref[...]

        def step(r, carry):
            v = acc[:, r + 1].reshape(2 * WD, C)
            v = (v - mean) * scale + shift
            v = v / (1.0 + jnp.exp(-v))
            out[:, r] = v.astype(BF16).reshape(2, WD, C)
            return carry

        lax.fori_loop(lo, hi, step, 0)

    def store(lo, hi, i):
        return pltpu.make_async_copy(
            out.at[:, pl.ds(lo, hi - lo)], o_ref.at[:, pl.ds(lo, hi - lo)], out_sem.at[i])

    @pl.when(second)
    def _():
        arrive(0)

    last_whole = 7

    def prev_step(s, carry):
        @pl.when(second & (s < last_whole))
        def _():
            arrive(s)

        p = other_p(s - 1)
        slot = jnp.where(first, 2, 0)

        @pl.when(second)
        def _():
            for side in (0, 1):
                strip(0, s - 1, p, side).wait_recv()
            for r in range(N):
                shifted(0, p + r)

        planes(slot, p, N, False, jnp.where(first, OFF, 0))

        @pl.when(second & (s == 4))
        def _():
            edges(0)

        @pl.when(second & (s == last_whole))
        def _():
            stats_begin()

        @pl.when(second & (s == last_whole + 1))
        def _():
            stats_middle()

        @pl.when(second & (s >= last_whole) & (s < CHUNKS))
        def _():
            arrive(s)

        @pl.when(second & (s == last_whole + 2))
        def _():
            stats_end()
            finish(0, SHARE_LO)
            finish(SHARE_HI, H)
            store(0, SHARE_LO, 0).start()
            store(SHARE_HI, H, 1).start()

        return carry

    lax.fori_loop(1, jnp.where(first, BACK, CHUNKS) + 1, prev_step, 0)

    @pl.when(first)
    def _():
        stats_begin()
        stats_middle()
        stats_end()
        finish(0, SHARE_LO)
        finish(SHARE_HI, H)
        store(0, SHARE_LO, 0).start()
        store(SHARE_HI, H, 1).start()

    finish(SHARE_LO, SHARE_HI)
    store(SHARE_LO, SHARE_HI, 2).start()

    for i in range(7):
        r1_copy(i).wait_send()
    for i in range(15):
        r2_copy(i).wait_send()
    for c in range(CHUNKS):
        for side in (0, 1):
            strip(1, c, c * N + 1, side).wait_send()

    def sent(c, carry):
        main(c, c * N).wait_send()
        return carry

    lax.fori_loop(0, jnp.where(first, CHUNKS, BACK), sent, 0)

    def passed(c, carry):
        for side in (0, 1):
            strip(0, c, 1 + c * N, side).wait_send()
        return carry

    lax.fori_loop(0, jnp.where(first, BACK, CHUNKS), passed, 0)
    for k in (1, 0):
        for way in (0, 1):
            ok = has_dn if way == 0 else has_up

            @pl.when(ok if k else ok & second)
            def _():
                for cp in rows(k, way):
                    cp.wait_send()
    store(0, SHARE_LO, 0).wait()
    store(SHARE_HI, H, 1).wait()
    store(SHARE_LO, SHARE_HI, 2).wait()


def body(latents, conv_weight, conv_bias, norm_gain, norm_shift):
    any_spec = pl.BlockSpec(memory_space=pl.ANY)
    vmem = pl.BlockSpec(memory_space=pltpu.VMEM)
    dma = pltpu.SemaphoreType.DMA
    halo = pltpu.VMEM((4, H + 2, WD, C), BF16)
    ends = pltpu.VMEM((4, H + 2, EDGE, C), BF16)
    return pl.pallas_call(
        kernel,
        out_shape=jax.ShapeDtypeStruct(latents.shape, BF16),
        in_specs=[any_spec, any_spec, vmem, vmem, vmem],
        out_specs=any_spec,
        scratch_shapes=[
            pltpu.VMEM((3, 3, 3 * C, C), BF16), halo, halo, halo, ends, ends,
            pltpu.VMEM((2, ACC_ROWS, WD, C), F32), pltpu.VMEM((2, H, WD, C), BF16),
            pltpu.VMEM((C, 128), F32), pltpu.VMEM((128, C), F32),
            pltpu.VMEM((8, C), F32), pltpu.VMEM((8, 128), F32),
            pltpu.VMEM((8, 8, 128), F32), pltpu.VMEM((16, 8, 128), F32),
            dma((CHUNKS,)), dma((3,)), dma((3,)), dma((CHUNKS,)), dma((CHUNKS,)),
            dma((2, CHUNKS, 2)), dma((2, CHUNKS, 2)), dma((2, 2, 3)), dma((2, 2, 3)),
            dma((7,)), dma((7,)), dma((15,)), dma((15,)),
        ],
        compiler_params=pltpu.CompilerParams(
            collective_id=0, has_side_effects=True, vmem_limit_bytes=56 * 2**20),
        cost_estimate=pl.CostEstimate(flops=20 * 10**9, bytes_accessed=16 * 2**20, transcendentals=10**6),
        name="conv_norm_silu",
    )(
        latents, conv_weight.reshape(3, 3, 3 * C, C), conv_bias.reshape(1, C),
        norm_gain.reshape(1, C), norm_shift.reshape(1, C))


def solution(mesh):
    spec = P("tm", "lat", "lon", None)
    return jax.shard_map(
        body, mesh=mesh, in_specs=(spec, P(), P(), P(), P()), out_specs=spec, check_vma=False)
```

```python
import functools

import jax
import jax.numpy as jnp
from jax import lax
from jax.experimental import pallas as pl
from jax.experimental.pallas import tpu as pltpu
from jax.sharding import PartitionSpec as P

MESH = pl.DeviceIdType.MESH
F32, BF16 = jnp.float32, jnp.bfloat16
HIGH = lax.Precision.HIGHEST

GROUPS = 32
C = 384
PER = C // GROUPS
H, WD = 40, 32
N = 4
CHUNKS = H // N

SHARE_LO, SHARE_HI = 15, 29
BACK = (SHARE_HI - SHARE_LO + 2) // N
BACK_ROW = SHARE_LO - 1
OFF = 30
ACC_ROWS = 62
LAST = 20
SKEW = BACK_ROW % N


def chunk_row(c):
    odd = c % 2
    half = c // 2
    return N * ((1 - odd) * half + odd * (CHUNKS - 1 - half))


def kernel(
    x_ref, w_ref, bias_in, gain_in, shift_in, o_ref,
    bias_ref, gain_ref, shift_ref,    wt, xm, xl, xr, cs, ch, cc, acc, g_in, g_out, aff, stat, r1, r2,
    loc_sem, w_sem, par_sem, main_s, main_r, strip_s, strip_r, own_s, own_r, end_s, end_r, back_s, back_r, row_s, row_r, r1_s, r1_r, r2_s, r2_r,
):
    tm, lat, lon = (lax.axis_index(a) for a in ("tm", "lat", "lon"))
    left, right = (lon + 15) % 16, (lon + 1) % 16
    z, yl = lon % 8, lon // 8
    first, second = tm == 0, tm == 1
    has_up, has_dn = lat > 0, lat < 3
    partner = (1 - tm, lat, lon)
    near = [(tm, lat, yl * 8 + (z + d) % 8) for d in range(1, 8)]
    far = [
        ((tm + a) % 2, (lat + b) % 4, ((yl + c) % 2) * 8 + z)
        for a in range(2) for b in range(4) for c in range(2)
    ][1:]
    corners = [(tm, (lat + b) % 4, l) for b in (0, 1, 3) for l in (left, right)]

    barrier = pltpu.get_barrier_semaphore()
    across = [(1 - tm, lat, right), (1 - tm, lat, left)]
    peers = far + near + corners + across
    for peer in peers:
        pl.semaphore_signal(barrier, inc=1, device_id=peer, device_id_type=MESH)

    def load_x(c):
        return pltpu.make_async_copy(
            x_ref.at[:, pl.ds(c * N, N)], xm.at[pl.ds(2, 2), pl.ds(c * N + 1, N)], loc_sem.at[c])

    def load_w(a):
        return pltpu.make_async_copy(w_ref.at[a], wt.at[a], w_sem.at[a])

    params = [
        pltpu.make_async_copy(src, dst, par_sem.at[i])
        for i, (src, dst) in enumerate(((bias_in, bias_ref), (gain_in, gain_ref), (shift_in, shift_ref)))]
    for cp in params:
        cp.start()
    for c in range(CHUNKS):
        load_x(c).start()
    for a in (2, 1, 0):
        load_w(a).start()

    row_i = lax.broadcasted_iota(jnp.int32, (C, 128), 0)
    lane_i = lax.broadcasted_iota(jnp.int32, (C, 128), 1)
    delta = row_i - PER * lane_i
    g_in[...] = jnp.where((delta >= 0) & (delta < PER), 1.0, 0.0)
    row_i = lax.broadcasted_iota(jnp.int32, (128, C), 0)
    lane_i = lax.broadcasted_iota(jnp.int32, (128, C), 1)
    delta = lane_i - PER * row_i
    g_out[...] = jnp.where((delta >= 0) & (delta < PER), 1.0, 0.0)

    def columns(k, c, p):
        ends = [xm[2 * k + f, p + r].astype(F32) for f in range(2) for r in range(N)]
        for i, v in enumerate(ends):
            cs[k, c, 0, i : i + 1] = v[WD - 1:]
            cs[k, c, 1, i : i + 1] = v[:1]

    def own_columns(c, carry):
        load_x(c).wait()
        columns(1, c, 1 + c * N)
        return carry

    lax.fori_loop(0, CHUNKS, own_columns, 0)

    pl.semaphore_wait(barrier, len(peers))

    def remote(src, dst, s, r, dev):
        return pltpu.make_async_remote_copy(
            src_ref=src, dst_ref=dst, send_sem=s, recv_sem=r, device_id=dev, device_id_type=MESH)

    def main(c, row):
        return remote(
            x_ref.at[:, pl.ds(row, N)], xm.at[pl.ds(0, 2), pl.ds(row + 1, N)],
            main_s.at[c], main_r.at[c], partner)

    def strip(c, side):
        return remote(cs.at[0, c, side], ch.at[0, c, side], strip_s.at[c, side], strip_r.at[c, side],
                      (tm, lat, (right, left)[side]))

    def own_strip(side):
        return remote(cs.at[1, :, side], ch.at[1, :, side], own_s.at[side], own_r.at[side],
                      (tm, lat, (right, left)[side]))

    def end_strip(side):
        return remote(cs.at[1, LAST // N, side], ch.at[0, CHUNKS - 1, side], end_s.at[side], end_r.at[side],
                      across[side])

    def back_strip():
        span = pl.ds(BACK_ROW // N, BACK + 1)
        return remote(ch.at[1, span], ch.at[0, span], back_s.at[0], back_r.at[0], partner)

    def rows(k, way):
        p = H if way == 0 else 1
        q = 0 if way == 0 else H + 1
        la = (lat + 1) % 4 if way == 0 else (lat + 3) % 4
        base = x_ref.at[:, pl.ds(p - 1, 1)] if k else xm.at[pl.ds(0, 2), pl.ds(p, 1)]
        c = 0 if way == 1 else CHUNKS - 1 if k else 1
        ss, rs = row_s.at[k, way], row_r.at[k, way]
        return [
            remote(base, xm.at[pl.ds(2 * k, 2), pl.ds(q, 1)], ss.at[0], rs.at[0], (tm, la, lon)),
            remote(cs.at[k, c, 0], cc.at[k, way, 0], ss.at[1], rs.at[1], (tm, la, right)),
            remote(cs.at[k, c, 1], cc.at[k, way, 1], ss.at[2], rs.at[2], (tm, la, left)),
        ]

    def rows_start(k, way):
        @pl.when(has_dn if way == 0 else has_up)
        def _():
            for cp in rows(k, way):
                cp.start()

    @pl.when(first)
    def _():
        for side in (0, 1):
            end_strip(side).start()
        main(0, chunk_row(0)).start()

    for side in (0, 1):
        own_strip(side).start()
    for way in (0, 1):
        rows_start(1, way)

    @pl.when(first)
    def _():
        for c in range(1, CHUNKS):
            main(c, chunk_row(c)).start()

    @pl.when(second)
    def _():
        for c in range(BACK):
            main(c, BACK_ROW + c * N).start()

    for cp in params:
        cp.wait()
    bias = jnp.broadcast_to(bias_ref[...].reshape(1, 1, C), (2, WD, C))

    def fill(r, carry):
        acc[:, r] = bias
        return carry

    lax.fori_loop(0, ACC_ROWS, fill, 0)

    def shifted(slot, p, ends, row):
        col = lax.broadcasted_iota(jnp.int32, (WD, C), 0)
        for f in range(2):
            v = xm[slot + f, p].astype(F32)
            i = f * N + row
            a, b = ends[0, i : i + 1], ends[1, i : i + 1]
            xl[slot + f, p] = jnp.where(col == 0, a, pltpu.roll(v, 1, 0)).astype(BF16)
            xr[slot + f, p] = jnp.where(col == WD - 1, b, pltpu.roll(v, WD - 1, 0)).astype(BF16)

    def planes(slot, p, n, own, off, taps=(0, 1, 2)):
        m = n * WD
        both = jnp.concatenate(
            [v[pl.ds(slot, 2), pl.ds(p, n)].reshape(2 * m, C) for v in (xl, xm, xr)], axis=1)
        one = both[:m] if own else both[m:]
        same, target = (2, 1) if own else (0, 0)
        for b in taps:
            rr = pl.ds(p + 1 - b + off, n)
            y = jnp.dot(both, wt[same, b], preferred_element_type=F32)
            acc[:, rr] += y.reshape(2, n, WD, C)
            y = jnp.dot(one, wt[1, b], preferred_element_type=F32)
            acc[target, rr] += y.reshape(n, WD, C)

    def edges(k):
        for way in (0, 1):
            @pl.when(has_up if way == 0 else has_dn)
            def _():
                for cp in rows(k, way):
                    cp.wait_recv()
                p = 0 if way == 0 else H + 1
                shifted(2 * k, p, cc.at[k, way], N - 1 if way == 0 else 0)
                planes(2 * k, p, 1, k == 1, 0, (0,) if way == 0 else (2,))

    def other_p(c):
        return jnp.where(first, BACK_ROW + 1 + c * N, chunk_row(c) + 1)

    def arrive(c):
        p = other_p(c)
        main(c, p - 1).wait_recv()

        @pl.when(second & (c < CHUNKS - 1))
        def _():
            columns(0, c, p)
            for side in (0, 1):
                strip(c, side).start()

        @pl.when(second & (c == 0))
        def _():
            rows_start(0, 1)

        @pl.when(second & (c == 1))
        def _():
            rows_start(0, 0)

    load_w(2).wait()
    load_w(1).wait()

    for side in (0, 1):
        own_strip(side).wait_recv()

    @pl.when(second)
    def _():
        back_strip().start()

    def own_step(i, carry):
        mine = i < CHUNKS
        j = jnp.maximum(i - CHUNKS, 0)
        slot = jnp.where(mine, 2, 0)
        p = jnp.where(mine, 1 + i * N, BACK_ROW + 1 + j * N)

        @pl.when(first & (i >= CHUNKS - 1) & (i < CHUNKS - 1 + BACK))
        def _():
            arrive(i - (CHUNKS - 1))

        @pl.when(i == CHUNKS)
        def _():
            back_strip().wait_recv()

        @pl.when(mine)
        def _():
            for r in range(N):
                shifted(2, p + r, ch.at[1, i], r)

        @pl.when(i >= CHUNKS)
        def _():
            for r in range(N):
                shifted(0, p + r, ch.at[0, BACK_ROW // N + j + (SKEW + r) // N], (SKEW + r) % N)

        planes(slot, p, N, True, jnp.where(mine, 0, OFF))
        return carry

    lax.fori_loop(0, jnp.where(first, CHUNKS + BACK, CHUNKS), own_step, 0)
    edges(1)
    load_w(0).wait()

    count = jnp.where(first, 54.0, 26.0) * (2 * WD * PER)
    other_count = jnp.where(first, 26.0, 54.0) * (2 * WD * PER)
    sub = lax.broadcasted_iota(jnp.int32, (8, 128), 0)

    def pack(mean, m2):
        return jnp.where(sub == 0, mean, jnp.where(sub == 1, m2, 0.0))

    def over_rows(f):
        def step(r, a):
            return a + f(acc[:, r].reshape(2 * WD // 8, 8, C)).sum(0)
        a = lax.fori_loop(1, jnp.where(first, 41, 1 + SHARE_LO), step, jnp.zeros((8, C), F32))
        a = lax.fori_loop(
            jnp.where(first, 1 + SHARE_LO + OFF, 1 + SHARE_HI), jnp.where(first, 1 + SHARE_HI + OFF, 41), step, a)
        return jnp.broadcast_to(a.sum(0, keepdims=True), (8, C))

    def group(v):
        return jnp.dot(v, g_in[...], precision=HIGH, preferred_element_type=F32)

    def channel(v):
        return jnp.dot(v, g_out[...], precision=HIGH, preferred_element_type=F32)

    def r1_copy(i):
        return remote(r1.at[0], r1.at[i + 1], r1_s.at[i], r1_r.at[i], near[i])

    def r2_copy(i):
        return remote(r2.at[0], r2.at[i + 1], r2_s.at[i], r2_r.at[i], far[i])

    def stats_begin():
        mean = group(over_rows(lambda v: v)) / count
        mean_c = channel(mean)
        m2 = group(over_rows(lambda v: (v - mean_c) * (v - mean_c)))
        r1[0] = pack(mean, m2)
        for i in range(7):
            r1_copy(i).start()

    def stats_middle():
        for i in range(7):
            r1_copy(i).wait_recv()
        means = [r1[i, 0:1] for i in range(8)]
        mean = sum(means) * 0.125
        m2 = sum(r1[i, 1:2] for i in range(8)) + count * sum((m - mean) * (m - mean) for m in means)
        r2[0] = pack(jnp.broadcast_to(mean, (8, 128)), jnp.broadcast_to(m2, (8, 128)))
        for i in range(15):
            r2_copy(i).start()

    def stats_end():
        for i in range(15):
            r2_copy(i).wait_recv()
        means = [r2[i, 0:1] for i in range(16)]
        mine, other = 8.0 * count, 8.0 * other_count
        total = 8.0 * (mine + other)
        mean = (mine * sum(means[:8]) + other * sum(means[8:])) / total
        m2 = sum(r2[i, 1:2] for i in range(16))
        m2 = m2 + mine * sum((m - mean) * (m - mean) for m in means[:8])
        m2 = m2 + other * sum((m - mean) * (m - mean) for m in means[8:])
        inv = lax.rsqrt(m2 / total + 1e-6)
        both = channel(pack(jnp.broadcast_to(mean, (8, 128)), jnp.broadcast_to(inv, (8, 128))))
        aff[0:1] = both[0:1]
        aff[1:2] = both[1:2] * gain_ref[...].reshape(1, C)

    def finish(lo, hi):
        mean, scale, shift = aff[0:1], aff[1:2], shift_ref[...].reshape(1, C)

        def step(r, carry):
            v = acc[:, r + 1].reshape(2 * WD, C)
            v = (v - mean) * scale + shift
            v = v / (1.0 + jnp.exp(-v))
            o_ref[:, r] = v.astype(BF16).reshape(2, WD, C)
            return carry

        lax.fori_loop(lo, hi, step, 0)

    @pl.when(second)
    def _():
        arrive(0)

    last_whole = 7

    def prev_step(s, carry):
        @pl.when(second & (s < last_whole))
        def _():
            arrive(s)

        p = other_p(s - 1)
        slot = jnp.where(first, 2, 0)

        @pl.when(second)
        def _():
            @pl.when(s < CHUNKS)
            def _():
                for side in (0, 1):
                    strip(s - 1, side).wait_recv()

            @pl.when(s == CHUNKS)
            def _():
                for side in (0, 1):
                    end_strip(side).wait_recv()

            for r in range(N):
                shifted(0, p + r, ch.at[0, s - 1], r)

        planes(slot, p, N, False, jnp.where(first, OFF, 0))

        @pl.when(second & (s == 4))
        def _():
            edges(0)

        @pl.when(second & (s == last_whole))
        def _():
            stats_begin()

        @pl.when(second & (s == last_whole + 1))
        def _():
            stats_middle()

        @pl.when(second & (s >= last_whole) & (s < CHUNKS))
        def _():
            arrive(s)

        @pl.when(second & (s == last_whole + 2))
        def _():
            stats_end()
            finish(0, SHARE_LO)
            finish(SHARE_HI, H)

        return carry

    lax.fori_loop(1, jnp.where(first, BACK, CHUNKS) + 1, prev_step, 0)

    @pl.when(first)
    def _():
        stats_begin()
        stats_middle()
        stats_end()
        finish(0, SHARE_LO)
        finish(SHARE_HI, H)

    finish(SHARE_LO, SHARE_HI)

    for i in range(7):
        r1_copy(i).wait_send()
    for i in range(15):
        r2_copy(i).wait_send()
    for side in (0, 1):
        own_strip(side).wait_send()

    def sent(c, carry):
        main(c, c * N).wait_send()
        return carry

    lax.fori_loop(0, jnp.where(first, CHUNKS, BACK), sent, 0)

    @pl.when(first)
    def _():
        for side in (0, 1):
            end_strip(side).wait_send()

    @pl.when(second)
    def _():
        back_strip().wait_send()
        for c in range(CHUNKS - 1):
            for side in (0, 1):
                strip(c, side).wait_send()

    for k in (1, 0):
        for way in (0, 1):
            ok = has_dn if way == 0 else has_up

            @pl.when(ok if k else ok & second)
            def _():
                for cp in rows(k, way):
                    cp.wait_send()


def body(latents, conv_weight, conv_bias, norm_gain, norm_shift):
    vmem = pl.BlockSpec(memory_space=pltpu.VMEM)
    hbm = pl.BlockSpec(memory_space=pltpu.HBM)
    dma = pltpu.SemaphoreType.DMA
    halo = pltpu.VMEM((4, H + 2, WD, C), BF16)
    ends = pltpu.VMEM((2, CHUNKS, 2, 2 * N, C), F32)
    return pl.pallas_call(
        kernel,
        out_shape=pltpu.VMEM(latents.shape, BF16),
        in_specs=[hbm] * 5,
        out_specs=vmem,
        scratch_shapes=[
            pltpu.VMEM((C,), F32), pltpu.VMEM((C,), F32), pltpu.VMEM((C,), F32),
            pltpu.VMEM((3, 3, 3 * C, C), BF16), halo, halo, halo, ends, ends, pltpu.VMEM((2, 2, 2, 2 * N, C), F32),
            pltpu.VMEM((2, ACC_ROWS, WD, C), F32),
            pltpu.VMEM((C, 128), F32), pltpu.VMEM((128, C), F32),
            pltpu.VMEM((8, C), F32), pltpu.VMEM((8, 128), F32),
            pltpu.VMEM((8, 8, 128), F32), pltpu.VMEM((16, 8, 128), F32),
            dma((CHUNKS,)), dma((3,)), dma((3,)), dma((CHUNKS,)), dma((CHUNKS,)),
            dma((CHUNKS, 2)), dma((CHUNKS, 2)), dma((2,)), dma((2,)), dma((2,)), dma((2,)), dma((1,)), dma((1,)),
            dma((2, 2, 3)), dma((2, 2, 3)),
            dma((7,)), dma((7,)), dma((15,)), dma((15,)),
        ],
        compiler_params=pltpu.CompilerParams(
            collective_id=0, has_side_effects=True, vmem_limit_bytes=48 * 2**20),
        cost_estimate=pl.CostEstimate(flops=20 * 10**9, bytes_accessed=16 * 2**20, transcendentals=10**6),
        name="conv_norm_silu",
    )(
        *(pltpu.with_memory_space_constraint(v, pltpu.HBM) for v in (
            latents, conv_weight.reshape(3, 3, 3 * C, C), conv_bias, norm_gain, norm_shift)))


def solution(mesh):
    spec = P("tm", "lat", "lon", None)
    return jax.shard_map(
        body, mesh=mesh, in_specs=(spec, P(), P(), P(), P()), out_specs=spec, check_vma=False)
```

```python
import functools

import jax
import jax.numpy as jnp
from jax import lax
from jax.experimental import pallas as pl
from jax.experimental.pallas import tpu as pltpu
from jax.sharding import PartitionSpec as P

MESH = pl.DeviceIdType.MESH
F32, BF16 = jnp.float32, jnp.bfloat16
HIGH = lax.Precision.HIGHEST

GROUPS = 32
C = 384
PER = C // GROUPS
H, WD = 40, 32
N = 4
CHUNKS = H // N

SHARE_LO, SHARE_HI = 15, 29
BACK = (SHARE_HI - SHARE_LO + 2) // N
BACK_ROW = SHARE_LO - 1
OFF = 30
ACC_ROWS = 62
BLOCK = 8
EARLY = 3
SKEW = BACK_ROW % N


def chunk_row(c):
    odd = c % 2
    half = c // 2
    return N * ((1 - odd) * half + odd * (CHUNKS - 1 - half))


def kernel(
    x_ref, w_ref, bias_in, gain_in, shift_in, o_ref,
    bias_ref, gain_ref, shift_ref,    wt, xm, xl, xr, cs, ch, cc, pk, pr, acc, g_in, g_out, aff, stat, r1, r2,
    loc_sem, w_sem, par_sem, main_s, main_r, own_s, own_r, pack_s, pack_r, back_s, back_r, row_s, row_r, r1_s, r1_r, r2_s, r2_r,
):
    tm, lat, lon = (lax.axis_index(a) for a in ("tm", "lat", "lon"))
    left, right = (lon + 15) % 16, (lon + 1) % 16
    z, yl = lon % 8, lon // 8
    first, second = tm == 0, tm == 1
    has_up, has_dn = lat > 0, lat < 3
    partner = (1 - tm, lat, lon)
    near = [(tm, lat, yl * 8 + (z + d) % 8) for d in range(1, 8)]
    far = [
        ((tm + a) % 2, (lat + b) % 4, ((yl + c) % 2) * 8 + z)
        for a in range(2) for b in range(4) for c in range(2)
    ][1:]
    corners = [(tm, (lat + b) % 4, l) for b in (0, 1, 3) for l in (left, right)]

    barrier = pltpu.get_barrier_semaphore()
    peers = far + near + corners
    for peer in peers:
        pl.semaphore_signal(barrier, inc=1, device_id=peer, device_id_type=MESH)

    def load_x(c):
        return pltpu.make_async_copy(
            x_ref.at[:, pl.ds(c * N, N)], xm.at[pl.ds(2, 2), pl.ds(c * N + 1, N)], loc_sem.at[c])

    def load_w(a):
        return pltpu.make_async_copy(w_ref.at[a], wt.at[:, :, pl.ds((2 - a) * C, C)], w_sem.at[a])

    params = [
        pltpu.make_async_copy(src, dst, par_sem.at[i])
        for i, (src, dst) in enumerate(((bias_in, bias_ref), (gain_in, gain_ref), (shift_in, shift_ref)))]
    for cp in params:
        cp.start()
    for c in range(CHUNKS):
        load_x(c).start()
    for a in (2, 1, 0):
        load_w(a).start()

    row_i = lax.broadcasted_iota(jnp.int32, (C, 128), 0)
    lane_i = lax.broadcasted_iota(jnp.int32, (C, 128), 1)
    delta = row_i - PER * lane_i
    g_in[...] = jnp.where((delta >= 0) & (delta < PER), 1.0, 0.0)
    row_i = lax.broadcasted_iota(jnp.int32, (128, C), 0)
    lane_i = lax.broadcasted_iota(jnp.int32, (128, C), 1)
    delta = lane_i - PER * row_i
    g_out[...] = jnp.where((delta >= 0) & (delta < PER), 1.0, 0.0)

    def columns(k, c, p):
        ends = [xm[2 * k + f, p + r].astype(F32) for f in range(2) for r in range(N)]
        for i, v in enumerate(ends):
            cs[k, c, 0, i : i + 1] = v[WD - 1:]
            cs[k, c, 1, i : i + 1] = v[:1]

    def own_columns(c, carry):
        load_x(c).wait()
        columns(1, c, 1 + c * N)
        return carry

    lax.fori_loop(0, CHUNKS, own_columns, 0)

    pl.semaphore_wait(barrier, len(peers))

    def remote(src, dst, s, r, dev):
        return pltpu.make_async_remote_copy(
            src_ref=src, dst_ref=dst, send_sem=s, recv_sem=r, device_id=dev, device_id_type=MESH)

    def main(c, row):
        return remote(
            x_ref.at[:, pl.ds(row, N)], xm.at[pl.ds(0, 2), pl.ds(row + 1, N)],
            main_s.at[c], main_r.at[c], partner)

    def own_strip(side):
        return remote(cs.at[1, :, side], ch.at[1, :, side], own_s.at[side], own_r.at[side],
                      (tm, lat, (right, left)[side]))

    def pack_strip():
        return remote(pk, pr, pack_s.at[0], pack_r.at[0], partner)

    def back_strip():
        span = pl.ds(BACK_ROW // N, BACK + 1)
        return remote(ch.at[1, span], ch.at[0, span], back_s.at[0], back_r.at[0], partner)

    def rows(k, way):
        p = H if way == 0 else 1
        q = 0 if way == 0 else H + 1
        la = (lat + 1) % 4 if way == 0 else (lat + 3) % 4
        base = x_ref.at[:, pl.ds(p - 1, 1)] if k else xm.at[pl.ds(0, 2), pl.ds(p, 1)]
        c = 0 if way == 1 else CHUNKS - 1 if k else 1
        ss, rs = row_s.at[k, way], row_r.at[k, way]
        return [
            remote(base, xm.at[pl.ds(2 * k, 2), pl.ds(q, 1)], ss.at[0], rs.at[0], (tm, la, lon)),
            remote(cs.at[k, c, 0], cc.at[k, way, 0], ss.at[1], rs.at[1], (tm, la, right)),
            remote(cs.at[k, c, 1], cc.at[k, way, 1], ss.at[2], rs.at[2], (tm, la, left)),
        ]

    def rows_start(k, way):
        @pl.when(has_dn if way == 0 else has_up)
        def _():
            for cp in rows(k, way):
                cp.start()

    for side in (0, 1):
        own_strip(side).start()

    @pl.when(first)
    def _():
        for c in range(EARLY):
            main(c, chunk_row(c)).start()

    for way in (0, 1):
        rows_start(1, way)

    @pl.when(second)
    def _():
        for c in range(2):
            main(c, BACK_ROW + c * N).start()

    for cp in params:
        cp.wait()

    def shifted(slot, p, ends, row):
        col = lax.broadcasted_iota(jnp.int32, (WD, C), 0)
        for f in range(2):
            v = xm[slot + f, p].astype(F32)
            i = f * N + row
            a, b = ends[0, i : i + 1], ends[1, i : i + 1]
            xl[slot + f, p] = jnp.where(col == 0, a, pltpu.roll(v, 1, 0)).astype(BF16)
            xr[slot + f, p] = jnp.where(col == WD - 1, b, pltpu.roll(v, WD - 1, 0)).astype(BF16)

    def taps(slot, p, n):
        return [v[slot, pl.ds(p, n)].reshape(n * WD, C) for v in (xl, xm, xr)]

    def own_planes(slot, h, off):
        ahead = [jnp.concatenate([v for b in range(3) for v in taps(slot + f, h + b, BLOCK)], axis=1) for f in range(2)]
        y = jnp.dot(ahead[0], wt[:, :, : 2 * C].reshape(9 * C, 2 * C), preferred_element_type=F32)
        z = jnp.dot(ahead[1], wt[:, :, :C].reshape(9 * C, C), preferred_element_type=F32)
        bias = bias_ref[...].reshape(1, C)
        rr = pl.ds(h + 1 + off, BLOCK)
        acc[0, rr] = (y[:, :C] + bias).reshape(BLOCK, WD, C)
        acc[1, rr] = (y[:, C:] + z + bias).reshape(BLOCK, WD, C)

    def prev_planes(slot, p, n, off, rows_b=(0, 1, 2)):
        older = jnp.concatenate(taps(slot, p, n), axis=1)
        newer = jnp.concatenate(taps(slot + 1, p, n), axis=1)
        for b in rows_b:
            rr = pl.ds(p + 1 - b + off, n)
            z = jnp.dot(older, wt[b, :, 2 * C :], preferred_element_type=F32)
            y = jnp.dot(newer, wt[b, :, C:], preferred_element_type=F32)
            acc[0, rr] += (y[:, :C] + z).reshape(n, WD, C)
            acc[1, rr] += y[:, C:].reshape(n, WD, C)

    def edge_rows(k):
        for way in (0, 1):
            ok = has_up if way == 0 else has_dn
            p = 0 if way == 0 else H + 1

            @pl.when(ok)
            def _():
                for cp in rows(k, way):
                    cp.wait_recv()
                shifted(2 * k, p, cc.at[k, way], N - 1 if way == 0 else 0)
                if k == 0:
                    prev_planes(0, p, 1, 0, (0,) if way == 0 else (2,))

            if k:
                @pl.when(jnp.logical_not(ok))
                def _():
                    for v in (xl, xm, xr):
                        v[pl.ds(2, 2), pl.ds(p, 1)] = jnp.zeros((2, 1, WD, C), BF16)

    def other_p(c):
        return jnp.where(first, BACK_ROW + 1 + c * N, chunk_row(c) + 1)

    for side in (0, 1):
        own_strip(side).wait_recv()

    @pl.when(second)
    def _():
        back_strip().start()
        for c in range(2, BACK):
            main(c, BACK_ROW + c * N).start()

    @pl.when(first)
    def _():
        for side in (0, 1):
            for t in range(CHUNKS // 2):
                pk[side, t] = jnp.concatenate([ch[1, 2 * t, side], ch[1, 2 * t + 1, side]], axis=0).astype(BF16)
        pack_strip().start()
        for c in range(EARLY, CHUNKS):
            main(c, chunk_row(c)).start()

    def own_shift(q):
        for r in range(N):
            shifted(2, 1 + q * N + r, ch.at[1, q], r)

    for q in range(3):
        own_shift(q)
    edge_rows(1)
    load_w(2).wait()
    load_w(1).wait()
    blocks = H // BLOCK

    def own_step(i, carry):
        mine = i < blocks

        @pl.when(i == blocks)
        def _():
            back_strip().wait_recv()
            for j in range(BACK):
                p = BACK_ROW + 1 + j * N
                main(j, p - 1).wait_recv()
                for r in range(N):
                    shifted(0, p + r, ch.at[0, BACK_ROW // N + j + (SKEW + r) // N], (SKEW + r) % N)

        own_planes(
            jnp.where(mine, 2, 0), jnp.where(mine, i * BLOCK, BACK_ROW + (i - blocks) * BLOCK), jnp.where(mine, 0, OFF))
        for k in (3, 4):
            own_shift(jnp.minimum(2 * i + k, CHUNKS - 1))
        return carry

    lax.fori_loop(0, jnp.where(first, blocks + BACK * N // BLOCK, blocks), own_step, 0)
    load_w(0).wait()

    count = jnp.where(first, 54.0, 26.0) * (2 * WD * PER)
    other_count = jnp.where(first, 26.0, 54.0) * (2 * WD * PER)
    sub = lax.broadcasted_iota(jnp.int32, (8, 128), 0)

    def pack(mean, m2):
        return jnp.where(sub == 0, mean, jnp.where(sub == 1, m2, 0.0))

    def over_rows(f):
        def step(r, a):
            return a + f(acc[:, r].reshape(2 * WD // 8, 8, C)).sum(0)
        a = lax.fori_loop(1, jnp.where(first, 41, 1 + SHARE_LO), step, jnp.zeros((8, C), F32))
        a = lax.fori_loop(
            jnp.where(first, 1 + SHARE_LO + OFF, 1 + SHARE_HI), jnp.where(first, 1 + SHARE_HI + OFF, 41), step, a)
        return jnp.broadcast_to(a.sum(0, keepdims=True), (8, C))

    def group(v):
        return jnp.dot(v, g_in[...], precision=HIGH, preferred_element_type=F32)

    def channel(v):
        return jnp.dot(v, g_out[...], precision=HIGH, preferred_element_type=F32)

    def r1_copy(i):
        return remote(r1.at[0], r1.at[i + 1], r1_s.at[i], r1_r.at[i], near[i])

    def r2_copy(i):
        return remote(r2.at[0], r2.at[i + 1], r2_s.at[i], r2_r.at[i], far[i])

    def stats_begin():
        mean = group(over_rows(lambda v: v)) / count
        mean_c = channel(mean)
        m2 = group(over_rows(lambda v: (v - mean_c) * (v - mean_c)))
        r1[0] = pack(mean, m2)
        for i in range(7):
            r1_copy(i).start()

    def stats_middle():
        for i in range(7):
            r1_copy(i).wait_recv()
        means = [r1[i, 0:1] for i in range(8)]
        mean = sum(means) * 0.125
        m2 = sum(r1[i, 1:2] for i in range(8)) + count * sum((m - mean) * (m - mean) for m in means)
        r2[0] = pack(jnp.broadcast_to(mean, (8, 128)), jnp.broadcast_to(m2, (8, 128)))
        for i in range(15):
            r2_copy(i).start()

    def stats_end():
        for i in range(15):
            r2_copy(i).wait_recv()
        means = [r2[i, 0:1] for i in range(16)]
        mine, other = 8.0 * count, 8.0 * other_count
        total = 8.0 * (mine + other)
        mean = (mine * sum(means[:8]) + other * sum(means[8:])) / total
        m2 = sum(r2[i, 1:2] for i in range(16))
        m2 = m2 + mine * sum((m - mean) * (m - mean) for m in means[:8])
        m2 = m2 + other * sum((m - mean) * (m - mean) for m in means[8:])
        inv = lax.rsqrt(m2 / total + 1e-6)
        both = channel(pack(jnp.broadcast_to(mean, (8, 128)), jnp.broadcast_to(inv, (8, 128))))
        aff[0:1] = both[0:1]
        aff[1:2] = both[1:2] * gain_ref[...].reshape(1, C)

    def finish(lo, hi):
        mean, scale, shift = aff[0:1], aff[1:2], shift_ref[...].reshape(1, C)

        def step(r, carry):
            v = acc[:, r + 1].reshape(2 * WD, C)
            v = (v - mean) * scale + shift
            v = v / (1.0 + jnp.exp(-v))
            o_ref[:, r] = v.astype(BF16).reshape(2, WD, C)
            return carry

        lax.fori_loop(lo, hi, step, 0)

    @pl.when(second)
    def _():
        pack_strip().wait_recv()
        for side in (0, 1):
            for t in range(CHUNKS // 2):
                v = pr[side, t].astype(F32)
                ch[0, 2 * t, side] = v[: 2 * N]
                ch[0, 2 * t + 1, side] = v[2 * N :]

    whole = 6

    def prev_step(c, carry):
        row = jnp.where(first, BACK_ROW + c * N, chunk_row(c))
        p = row + 1
        slot = jnp.where(first, 2, 0)

        @pl.when(second)
        def _():
            main(c, row).wait_recv()

            @pl.when(c < 2)
            def _():
                columns(0, c, p)

            @pl.when(c == 0)
            def _():
                rows_start(0, 1)

            @pl.when(c == 1)
            def _():
                rows_start(0, 0)

            @pl.when(c == whole - 1)
            def _():
                edge_rows(0)

            for r in range(N):
                shifted(0, p + r, ch.at[0, row // N], r)

        prev_planes(slot, p, N, jnp.where(first, OFF, 0))

        @pl.when(second & (c == whole))
        def _():
            stats_begin()

        @pl.when(second & (c == whole + 1))
        def _():
            stats_middle()

        @pl.when(second & (c == whole + 2))
        def _():
            stats_end()
            finish(0, SHARE_LO)
            finish(SHARE_HI, H)

        return carry

    lax.fori_loop(0, jnp.where(first, BACK, CHUNKS), prev_step, 0)

    @pl.when(first)
    def _():
        stats_begin()
        stats_middle()
        stats_end()
        finish(0, SHARE_LO)
        finish(SHARE_HI, H)

    finish(SHARE_LO, SHARE_HI)

    for i in range(7):
        r1_copy(i).wait_send()
    for i in range(15):
        r2_copy(i).wait_send()
    for side in (0, 1):
        own_strip(side).wait_send()

    def sent(c, carry):
        main(c, c * N).wait_send()
        return carry

    lax.fori_loop(0, jnp.where(first, CHUNKS, BACK), sent, 0)

    @pl.when(first)
    def _():
        pack_strip().wait_send()

    @pl.when(second)
    def _():
        back_strip().wait_send()

    for k in (1, 0):
        for way in (0, 1):
            ok = has_dn if way == 0 else has_up

            @pl.when(ok if k else ok & second)
            def _():
                for cp in rows(k, way):
                    cp.wait_send()


def body(latents, conv_weight, conv_bias, norm_gain, norm_shift):
    vmem = pl.BlockSpec(memory_space=pltpu.VMEM)
    hbm = pl.BlockSpec(memory_space=pltpu.HBM)
    dma = pltpu.SemaphoreType.DMA
    halo = pltpu.VMEM((4, H + 2, WD, C), BF16)
    ends = pltpu.VMEM((2, CHUNKS, 2, 2 * N, C), F32)
    packed = pltpu.VMEM((2, CHUNKS // 2, 4 * N, C), BF16)
    return pl.pallas_call(
        kernel,
        out_shape=pltpu.VMEM(latents.shape, BF16),
        in_specs=[hbm] * 5,
        out_specs=vmem,
        scratch_shapes=[
            pltpu.VMEM((C,), F32), pltpu.VMEM((C,), F32), pltpu.VMEM((C,), F32),
            pltpu.VMEM((3, 3 * C, 3 * C), BF16), halo, halo, halo, ends, ends, pltpu.VMEM((2, 2, 2, 2 * N, C), F32),
            packed, packed,
            pltpu.VMEM((2, ACC_ROWS, WD, C), F32),
            pltpu.VMEM((C, 128), F32), pltpu.VMEM((128, C), F32),
            pltpu.VMEM((8, C), F32), pltpu.VMEM((8, 128), F32),
            pltpu.VMEM((8, 8, 128), F32), pltpu.VMEM((16, 8, 128), F32),
            dma((CHUNKS,)), dma((3,)), dma((3,)), dma((CHUNKS,)), dma((CHUNKS,)),
            dma((2,)), dma((2,)), dma((1,)), dma((1,)), dma((1,)), dma((1,)),
            dma((2, 2, 3)), dma((2, 2, 3)),
            dma((7,)), dma((7,)), dma((15,)), dma((15,)),
        ],
        compiler_params=pltpu.CompilerParams(
            collective_id=0, has_side_effects=True, vmem_limit_bytes=48 * 2**20),
        cost_estimate=pl.CostEstimate(flops=20 * 10**9, bytes_accessed=16 * 2**20, transcendentals=10**6),
        name="conv_norm_silu",
    )(
        *(pltpu.with_memory_space_constraint(v, pltpu.HBM) for v in (
            latents, conv_weight.reshape(3, 3, 3 * C, C), conv_bias, norm_gain, norm_shift)))


def solution(mesh):
    spec = P("tm", "lat", "lon", None)
    return jax.shard_map(
        body, mesh=mesh, in_specs=(spec, P(), P(), P(), P()), out_specs=spec, check_vma=False)
```

```python
import functools

import jax
import jax.numpy as jnp
from jax import lax
from jax.experimental import pallas as pl
from jax.experimental.pallas import tpu as pltpu
from jax.sharding import PartitionSpec as P

MESH = pl.DeviceIdType.MESH
F32, BF16 = jnp.float32, jnp.bfloat16
HIGH = lax.Precision.HIGHEST

GROUPS = 32
C = 384
PER = C // GROUPS
H, WD = 40, 32
N = 4
CHUNKS = H // N

SHARE_LO, SHARE_HI = 11, 29
BACK = (SHARE_HI - SHARE_LO + 2) // N
BACK_ROW = SHARE_LO - 1
OFF = 33
ACC_ROWS = 64
BLOCK = 8
SHARE_BLOCK = 10
SHARED = SHARE_HI - SHARE_LO
EARLY = 3
SKEW = BACK_ROW % N
PAIRS = CHUNKS // 2
END_LO, END_HI = 19, 25
PIVOT = 6


def chunk_row(c):
    odd = c % 2
    half = c // 2
    return N * ((1 - odd) * half + odd * (CHUNKS - 1 - half))


def kernel(
    x_ref, w_ref, bias_in, gain_in, shift_in, o_ref,
    bias_ref, gain_ref, shift_ref,    wt, xm, xl, xr, ends, cs, ph, ch, cc, acc, g_in, g_out, aff, stat, r1, r2,
    loc_sem, w_sem, par_sem, main_s, main_r, own_s, own_r, pack_s, pack_r, back_s, back_r, row_s, row_r, r1_s, r1_r, r2_s, r2_r,
):
    tm, lat, lon = (lax.axis_index(a) for a in ("tm", "lat", "lon"))
    left, right = (lon + 15) % 16, (lon + 1) % 16
    z, yl = lon % 8, lon // 8
    first, second = tm == 0, tm == 1
    has_up, has_dn = lat > 0, lat < 3
    partner = (1 - tm, lat, lon)
    near = [(tm, lat, yl * 8 + (z + d) % 8) for d in range(1, 8)]
    far = [
        ((tm + a) % 2, (lat + b) % 4, ((yl + c) % 2) * 8 + z)
        for a in range(2) for b in range(4) for c in range(2)
    ][1:]

    barrier = pltpu.get_barrier_semaphore()
    for peer in far + near:
        pl.semaphore_signal(barrier, inc=1, device_id=peer, device_id_type=MESH)

    @pl.when(z == 7)
    def _():
        pl.semaphore_signal(barrier, inc=1, device_id=(tm, lat, right), device_id_type=MESH)

    @pl.when(z == 0)
    def _():
        pl.semaphore_signal(barrier, inc=1, device_id=(tm, lat, left), device_id_type=MESH)

    def load_x(c):
        return pltpu.make_async_copy(
            x_ref.at[:, pl.ds(c * N, N)], xm.at[pl.ds(2, 2), pl.ds(c * N + 1, N)], loc_sem.at[c])

    def load_w(a):
        return pltpu.make_async_copy(w_ref.at[a], wt.at[:, :, pl.ds((2 - a) * C, C)], w_sem.at[a])

    params = [
        pltpu.make_async_copy(src, dst, par_sem.at[i])
        for i, (src, dst) in enumerate(((bias_in, bias_ref), (gain_in, gain_ref), (shift_in, shift_ref)))]
    for cp in params:
        cp.start()
    for c in range(CHUNKS):
        load_x(c).start()
    for a in (2, 1, 0):
        load_w(a).start()

    row_i = lax.broadcasted_iota(jnp.int32, (C, 128), 0)
    lane_i = lax.broadcasted_iota(jnp.int32, (C, 128), 1)
    delta = row_i - PER * lane_i
    g_in[...] = jnp.where((delta >= 0) & (delta < PER), 1.0, 0.0)
    row_i = lax.broadcasted_iota(jnp.int32, (128, C), 0)
    lane_i = lax.broadcasted_iota(jnp.int32, (128, C), 1)
    delta = lane_i - PER * row_i
    g_out[...] = jnp.where((delta >= 0) & (delta < PER), 1.0, 0.0)

    def own_columns(t, carry):
        for q in range(2):
            load_x(2 * t + q).wait()
            for f in range(2):
                for r in range(N):
                    v = xm[2 + f, (2 * t + q) * N + 1 + r].astype(F32)
                    i = (2 * q + f) * N + r
                    ends[0, i : i + 1] = v[WD - 1:]
                    ends[1, i : i + 1] = v[:1]
        for side in (0, 1):
            cs[side, t] = ends[side].astype(BF16)
        return carry

    lax.fori_loop(0, PAIRS, own_columns, 0)

    pl.semaphore_wait(barrier, len(far + near) + jnp.where((z == 0) | (z == 7), 1, 0))

    def remote(src, dst, s, r, dev):
        return pltpu.make_async_remote_copy(
            src_ref=src, dst_ref=dst, send_sem=s, recv_sem=r, device_id=dev, device_id_type=MESH)

    def main(c, row):
        return remote(
            x_ref.at[:, pl.ds(row, N)], xm.at[pl.ds(0, 2), pl.ds(row + 1, N)],
            main_s.at[c], main_r.at[c], partner)

    def own_strip(side):
        return remote(cs.at[side], ph.at[1, side], own_s.at[side], own_r.at[side], (tm, lat, (right, left)[side]))

    def pack_strip():
        return remote(ph.at[1], ph.at[0], pack_s.at[0], pack_r.at[0], partner)

    def back_strip():
        span = pl.ds(BACK_ROW // (2 * N), (BACK_ROW + BACK * N - 1) // (2 * N) - BACK_ROW // (2 * N) + 1)
        return remote(ph.at[1, :, span], ph.at[0, :, span], back_s.at[0], back_r.at[0], partner)

    def unpack(k, pairs):
        for t in pairs:
            for side in (0, 1):
                v = ph[k, side, t].astype(F32)
                ch[k, 2 * t, side] = v[: 2 * N]
                ch[k, 2 * t + 1, side] = v[2 * N :]

    def rows(k, way, part):
        la = (lat + 1) % 4 if way == 0 else (lat + 3) % 4
        sems = (row_s.at[k, way, part], row_r.at[k, way, part], (tm, la, lon))
        if part:
            return remote(ch.at[k, 0 if way == 1 else CHUNKS - 1], cc.at[k, way], *sems)
        p = H if way == 0 else 1
        q = 0 if way == 0 else H + 1
        base = x_ref.at[:, pl.ds(p - 1, 1)] if k else xm.at[pl.ds(0, 2), pl.ds(p, 1)]
        return remote(base, xm.at[pl.ds(2 * k, 2), pl.ds(q, 1)], *sems)

    def rows_start(k, way, part):
        @pl.when(has_dn if way == 0 else has_up)
        def _():
            rows(k, way, part).start()

    for side in (0, 1):
        own_strip(side).start()

    @pl.when(first)
    def _():
        for c in range(EARLY):
            main(c, chunk_row(c)).start()

    for way in (0, 1):
        rows_start(1, way, 0)

    @pl.when(second)
    def _():
        for c in range(2):
            main(c, BACK_ROW + c * N).start()

    for cp in params:
        cp.wait()

    def shifted(slot, p, ends, row):
        col = lax.broadcasted_iota(jnp.int32, (WD, C), 0)
        for f in range(2):
            v = xm[slot + f, p].astype(F32)
            i = f * N + row
            a, b = ends[0, i : i + 1], ends[1, i : i + 1]
            xl[slot + f, p] = jnp.where(col == 0, a, pltpu.roll(v, 1, 0)).astype(BF16)
            xr[slot + f, p] = jnp.where(col == WD - 1, b, pltpu.roll(v, WD - 1, 0)).astype(BF16)

    def taps(slot, p, n):
        return [v[slot, pl.ds(p, n)].reshape(n * WD, C) for v in (xl, xm, xr)]

    def own_planes(slot, h, n, off, add):
        ahead = [jnp.concatenate([v for b in range(3) for v in taps(slot + f, h + b, n)], axis=1) for f in range(2)]
        y = jnp.dot(ahead[0], wt[:, :, : 2 * C].reshape(9 * C, 2 * C), preferred_element_type=F32)
        z = jnp.dot(ahead[1], wt[:, :, :C].reshape(9 * C, C), preferred_element_type=F32)
        rr = pl.ds(h + 1 + off, n)
        if add:
            acc[0, rr] += y[:, :C].reshape(n, WD, C)
            acc[1, rr] += (y[:, C:] + z).reshape(n, WD, C)
        else:
            bias = bias_ref[...].reshape(1, C)
            acc[0, rr] = (y[:, :C] + bias).reshape(n, WD, C)
            acc[1, rr] = (y[:, C:] + z + bias).reshape(n, WD, C)

    def prev_planes(slot, p, n, off, rows_b=(0, 1, 2)):
        older = jnp.concatenate(taps(slot, p, n), axis=1)
        newer = jnp.concatenate(taps(slot + 1, p, n), axis=1)
        for b in rows_b:
            rr = pl.ds(p + 1 - b + off, n)
            z = jnp.dot(older, wt[b, :, 2 * C :], preferred_element_type=F32)
            y = jnp.dot(newer, wt[b, :, C:], preferred_element_type=F32)
            acc[0, rr] += (y[:, :C] + z).reshape(n, WD, C)
            acc[1, rr] += y[:, C:].reshape(n, WD, C)

    def prev_block(slot, h, n, off):
        ahead = [jnp.concatenate([v for b in range(3) for v in taps(slot + f, h + b, n)], axis=1) for f in range(2)]
        z = jnp.dot(ahead[0], wt[:, :, 2 * C :].reshape(9 * C, C), preferred_element_type=F32)
        y = jnp.dot(ahead[1], wt[:, :, C:].reshape(9 * C, 2 * C), preferred_element_type=F32)
        bias = bias_ref[...].reshape(1, C)
        rr = pl.ds(h + 1 + off, n)
        acc[0, rr] = (y[:, :C] + z + bias).reshape(n, WD, C)
        acc[1, rr] = (y[:, C:] + bias).reshape(n, WD, C)

    def edge_rows(k):
        for way in (0, 1):
            ok = has_up if way == 0 else has_dn
            p = 0 if way == 0 else H + 1

            @pl.when(ok)
            def _():
                for part in (0, 1):
                    rows(k, way, part).wait_recv()
                shifted(2 * k, p, cc.at[k, way], N - 1 if way == 0 else 0)
                if k == 0:
                    prev_planes(0, p, 1, 0, (0,) if way == 0 else (2,))

            if k:
                @pl.when(jnp.logical_not(ok))
                def _():
                    for v in (xl, xm, xr):
                        v[pl.ds(2, 2), pl.ds(p, 1)] = jnp.zeros((2, 1, WD, C), BF16)

    def other_p(c):
        return jnp.where(first, BACK_ROW + 1 + c * N, chunk_row(c) + 1)

    for side in (0, 1):
        own_strip(side).wait_recv()

    @pl.when(second)
    def _():
        back_strip().start()
        for c in range(2, BACK):
            main(c, BACK_ROW + c * N).start()

    @pl.when(first)
    def _():
        pack_strip().start()
        for c in range(EARLY, CHUNKS):
            main(c, chunk_row(c)).start()

    unpack(1, range(PAIRS))
    for way in (0, 1):
        rows_start(1, way, 1)

    def own_shift(q):
        for r in range(N):
            shifted(2, 1 + q * N + r, ch.at[1, q], r)

    for q in range(1, 5):
        own_shift(q)
    load_w(2).wait()
    load_w(1).wait()
    blocks = H // BLOCK

    def own_step(i, carry):
        @pl.when(i == blocks - 2)
        def _():
            edge_rows(1)

        own_planes(2, (i + 1) % blocks * BLOCK, BLOCK, 0, False)
        for k in (5, 6):
            own_shift((2 * i + k) % CHUNKS)
        return carry

    lax.fori_loop(0, blocks, own_step, 0)
    load_w(0).wait()

    count = jnp.where(first, float(H + SHARED), float(H - SHARED)) * (2 * WD * PER)
    other_count = jnp.where(first, float(H - SHARED), float(H + SHARED)) * (2 * WD * PER)
    sub = lax.broadcasted_iota(jnp.int32, (8, 128), 0)

    def pack(mean, m2):
        return jnp.where(sub == 0, mean, jnp.where(sub == 1, m2, 0.0))

    def over_rows():
        pivot = aff[8:16]

        def step(r, sums):
            d = acc[:, r].reshape(2 * WD // 8, 8, C) - pivot
            return sums[0] + d.sum(0), sums[1] + (d * d).sum(0)

        sums = (jnp.zeros((8, C), F32), jnp.zeros((8, C), F32))
        sums = lax.fori_loop(1, jnp.where(first, 1 + H, 1 + SHARE_LO), step, sums)
        sums = lax.fori_loop(
            jnp.where(first, 1 + SHARE_LO + OFF, 1 + SHARE_HI), jnp.where(first, 1 + SHARE_HI + OFF, 1 + H), step, sums)
        return [jnp.broadcast_to(v.sum(0, keepdims=True), (8, C)) for v in sums]

    def group(v):
        return jnp.dot(v, g_in[...], precision=HIGH, preferred_element_type=F32)

    def channel(v):
        return jnp.dot(v, g_out[...], precision=HIGH, preferred_element_type=F32)

    def r1_copy(i):
        return remote(r1.at[0], r1.at[i + 1], r1_s.at[i], r1_r.at[i], near[i])

    def r2_copy(i):
        return remote(r2.at[0], r2.at[i + 1], r2_s.at[i], r2_r.at[i], far[i])

    def stats_pivot():
        v = acc[:, PIVOT].reshape(2 * WD // 8, 8, C).sum(0).sum(0, keepdims=True)
        mean = group(jnp.broadcast_to(v, (8, C))) * (1.0 / (2 * WD * PER))
        stat[...] = mean
        aff[8:16] = channel(mean)

    def stats_begin():
        s1, s2 = over_rows()
        sums = group(jnp.where(lax.broadcasted_iota(jnp.int32, (8, C), 0) == 0, s1, s2))
        shift = sums[0:1] / count
        m2 = jnp.maximum(sums[1:2] - sums[0:1] * shift, 0.0)
        r1[0] = pack(stat[...] + shift, jnp.broadcast_to(m2, (8, 128)))
        for i in range(7):
            r1_copy(i).start()

    def stats_middle():
        for i in range(7):
            r1_copy(i).wait_recv()
        means = [r1[i, 0:1] for i in range(8)]
        mean = sum(means) * 0.125
        m2 = sum(r1[i, 1:2] for i in range(8)) + count * sum((m - mean) * (m - mean) for m in means)
        r2[0] = pack(jnp.broadcast_to(mean, (8, 128)), jnp.broadcast_to(m2, (8, 128)))
        for i in range(15):
            r2_copy(i).start()

    def stats_end():
        for i in range(15):
            r2_copy(i).wait_recv()
        means = [r2[i, 0:1] for i in range(16)]
        mine, other = 8.0 * count, 8.0 * other_count
        total = 8.0 * (mine + other)
        mean = (mine * sum(means[:8]) + other * sum(means[8:])) / total
        m2 = sum(r2[i, 1:2] for i in range(16))
        m2 = m2 + mine * sum((m - mean) * (m - mean) for m in means[:8])
        m2 = m2 + other * sum((m - mean) * (m - mean) for m in means[8:])
        inv = lax.rsqrt(m2 / total + 1e-6)
        both = channel(pack(jnp.broadcast_to(mean, (8, 128)), jnp.broadcast_to(inv, (8, 128))))
        aff[0:1] = both[0:1]
        aff[1:2] = both[1:2] * gain_ref[...].reshape(1, C)

    def finish(lo, hi):
        mean, scale, shift = aff[0:1], aff[1:2], shift_ref[...].reshape(1, C)

        def step(r, carry):
            v = acc[:, r + 1].reshape(2 * WD, C)
            v = (v - mean) * scale + shift
            v = v / (1.0 + jnp.exp(-v))
            o_ref[:, r] = v.astype(BF16).reshape(2, WD, C)
            return carry

        lax.fori_loop(lo, hi, step, 0)

    @pl.when(second)
    def _():
        pack_strip().wait_recv()
        unpack(0, range(PAIRS))
        for way in (0, 1):
            rows_start(0, way, 1)

    whole = 5

    def prev_step(c, carry):
        row = chunk_row(c)
        p = row + 1
        main(c, row).wait_recv()

        @pl.when(c == 0)
        def _():
            rows_start(0, 1, 0)

        @pl.when(c == 1)
        def _():
            rows_start(0, 0, 0)

        @pl.when(c == whole - 1)
        def _():
            edge_rows(0)
            stats_pivot()

        for r in range(N):
            shifted(0, p + r, ch.at[0, row // N], r)
        prev_planes(0, p, N, 0)

        @pl.when(c == whole)
        def _():
            stats_begin()

        @pl.when(c == whole + 1)
        def _():
            stats_middle()

        @pl.when(c == CHUNKS - 2)
        def _():
            stats_end()
            finish(0, END_LO)
            finish(END_HI, H)

        return carry

    @pl.when(second)
    def _():
        lax.fori_loop(0, CHUNKS, prev_step, 0)
        finish(END_LO, END_HI)

    @pl.when(first)
    def _():
        def shared_prev(i, carry):
            prev_block(2, BACK_ROW + i * SHARE_BLOCK, SHARE_BLOCK, OFF)
            return carry

        lax.fori_loop(0, BACK * N // SHARE_BLOCK, shared_prev, 0)
        stats_pivot()
        back_strip().wait_recv()
        unpack(0, range(BACK_ROW // (2 * N), (BACK_ROW + BACK * N - 1) // (2 * N) + 1))
        for j in range(BACK):
            p = BACK_ROW + 1 + j * N
            main(j, p - 1).wait_recv()
            for r in range(N):
                shifted(0, p + r, ch.at[0, BACK_ROW // N + j + (SKEW + r) // N], (SKEW + r) % N)

        def shared_step(i, carry):
            own_planes(0, BACK_ROW + i * SHARE_BLOCK, SHARE_BLOCK, OFF, True)
            return carry

        lax.fori_loop(0, BACK * N // SHARE_BLOCK, shared_step, 0)
        stats_begin()
        stats_middle()
        stats_end()
        finish(0, H)

    for i in range(7):
        r1_copy(i).wait_send()
    for i in range(15):
        r2_copy(i).wait_send()
    for side in (0, 1):
        own_strip(side).wait_send()

    def sent(c, carry):
        main(c, c * N).wait_send()
        return carry

    lax.fori_loop(0, jnp.where(first, CHUNKS, BACK), sent, 0)

    @pl.when(first)
    def _():
        pack_strip().wait_send()

    @pl.when(second)
    def _():
        back_strip().wait_send()

    for k in (1, 0):
        for way in (0, 1):
            ok = has_dn if way == 0 else has_up

            @pl.when(ok if k else ok & second)
            def _():
                for part in (0, 1):
                    rows(k, way, part).wait_send()


def body(latents, conv_weight, conv_bias, norm_gain, norm_shift):
    vmem = pl.BlockSpec(memory_space=pltpu.VMEM)
    hbm = pl.BlockSpec(memory_space=pltpu.HBM)
    dma = pltpu.SemaphoreType.DMA
    halo = pltpu.VMEM((4, H + 2, WD, C), BF16)
    packed = (2, PAIRS, 4 * N, C)
    return pl.pallas_call(
        kernel,
        out_shape=pltpu.VMEM(latents.shape, BF16),
        in_specs=[hbm] * 5,
        out_specs=vmem,
        scratch_shapes=[
            pltpu.VMEM((C,), F32), pltpu.VMEM((C,), F32), pltpu.VMEM((C,), F32),
            pltpu.VMEM((3, 3 * C, 3 * C), BF16), halo, halo, halo,
            pltpu.VMEM((2, 4 * N, C), F32), pltpu.VMEM(packed, BF16), pltpu.VMEM((2,) + packed, BF16),
            pltpu.VMEM((2, CHUNKS, 2, 2 * N, C), F32), pltpu.VMEM((2, 2, 2, 2 * N, C), F32),
            pltpu.VMEM((2, ACC_ROWS, WD, C), F32),
            pltpu.VMEM((C, 128), F32), pltpu.VMEM((128, C), F32),
            pltpu.VMEM((16, C), F32), pltpu.VMEM((8, 128), F32),
            pltpu.VMEM((8, 8, 128), F32), pltpu.VMEM((16, 8, 128), F32),
            dma((CHUNKS,)), dma((3,)), dma((3,)), dma((CHUNKS,)), dma((CHUNKS,)),
            dma((2,)), dma((2,)), dma((1,)), dma((1,)), dma((1,)), dma((1,)),
            dma((2, 2, 2)), dma((2, 2, 2)),
            dma((7,)), dma((7,)), dma((15,)), dma((15,)),
        ],
        compiler_params=pltpu.CompilerParams(
            collective_id=0, has_side_effects=True, vmem_limit_bytes=48 * 2**20),
        cost_estimate=pl.CostEstimate(flops=20 * 10**9, bytes_accessed=16 * 2**20, transcendentals=10**6),
        name="conv_norm_silu",
    )(
        *(pltpu.with_memory_space_constraint(v, pltpu.HBM) for v in (
            latents, conv_weight.reshape(3, 3, 3 * C, C), conv_bias, norm_gain, norm_shift)))


def solution(mesh):
    spec = P("tm", "lat", "lon", None)
    return jax.shard_map(
        body, mesh=mesh, in_specs=(spec, P(), P(), P(), P()), out_specs=spec, check_vma=False)
```

```python
import functools

import jax
import jax.numpy as jnp
from jax import lax
from jax.experimental import pallas as pl
from jax.experimental.pallas import tpu as pltpu
from jax.sharding import PartitionSpec as P

MESH = pl.DeviceIdType.MESH
F32, BF16 = jnp.float32, jnp.bfloat16
HIGH = lax.Precision.HIGHEST

GROUPS = 32
C = 384
PER = C // GROUPS
H, WD = 40, 32
N = 4
CHUNKS = H // N

SHARE_LO, SHARE_HI = 11, 29
BACK = (SHARE_HI - SHARE_LO + 2) // N
BACK_ROW = SHARE_LO - 1
OFF = 33
ACC_ROWS = 64
BLOCK = 8
SHARE_BLOCK = 10
SHARED = SHARE_HI - SHARE_LO
EARLY = 3
SKEW = BACK_ROW % N
PAIRS = CHUNKS // 2
END_LO, END_HI = 19, 25
PIVOT = 6


def chunk_row(c):
    odd = c % 2
    half = c // 2
    return N * ((1 - odd) * half + odd * (CHUNKS - 1 - half))


def kernel(
    x_ref, w_ref, bias_in, gain_in, shift_in, o_ref,
    bias_ref, gain_ref, shift_ref,    wt, xm, xl, xr, ends, cs, ph, ch, cc, acc, g_in, g_out, aff, stat, r1, r2,
    loc_sem, w_sem, par_sem, main_s, main_r, own_s, own_r, pack_s, pack_r, back_s, back_r, row_s, row_r, r1_s, r1_r, r2_s, r2_r,
):
    tm, lat, lon = (lax.axis_index(a) for a in ("tm", "lat", "lon"))
    left, right = (lon + 15) % 16, (lon + 1) % 16
    z, yl = lon % 8, lon // 8
    first, second = tm == 0, tm == 1
    has_up, has_dn = lat > 0, lat < 3
    partner = (1 - tm, lat, lon)
    near = [(tm, lat, yl * 8 + (z + d) % 8) for d in range(1, 8)]
    far = [
        ((tm + a) % 2, (lat + b) % 4, ((yl + c) % 2) * 8 + z)
        for a in range(2) for b in range(4) for c in range(2)
    ][1:]

    barrier = pltpu.get_barrier_semaphore()
    for peer in far + near:
        pl.semaphore_signal(barrier, inc=1, device_id=peer, device_id_type=MESH)

    @pl.when(z == 7)
    def _():
        pl.semaphore_signal(barrier, inc=1, device_id=(tm, lat, right), device_id_type=MESH)

    @pl.when(z == 0)
    def _():
        pl.semaphore_signal(barrier, inc=1, device_id=(tm, lat, left), device_id_type=MESH)

    def load_x(c):
        return pltpu.make_async_copy(
            x_ref.at[:, pl.ds(c * N, N)], xm.at[pl.ds(2, 2), pl.ds(c * N + 1, N)], loc_sem.at[c])

    def load_w(a):
        return pltpu.make_async_copy(w_ref.at[a], wt.at[:, :, pl.ds((2 - a) * C, C)], w_sem.at[a])

    params = [
        pltpu.make_async_copy(src, dst, par_sem.at[i])
        for i, (src, dst) in enumerate(((bias_in, bias_ref), (gain_in, gain_ref), (shift_in, shift_ref)))]
    for cp in params:
        cp.start()
    for c in range(CHUNKS):
        load_x(c).start()
    for a in (2, 1, 0):
        load_w(a).start()

    row_i = lax.broadcasted_iota(jnp.int32, (C, 128), 0)
    lane_i = lax.broadcasted_iota(jnp.int32, (C, 128), 1)
    delta = row_i - PER * lane_i
    g_in[...] = jnp.where((delta >= 0) & (delta < PER), 1.0, 0.0)
    row_i = lax.broadcasted_iota(jnp.int32, (128, C), 0)
    lane_i = lax.broadcasted_iota(jnp.int32, (128, C), 1)
    delta = lane_i - PER * row_i
    g_out[...] = jnp.where((delta >= 0) & (delta < PER), 1.0, 0.0)

    def own_columns(t, carry):
        for q in range(2):
            load_x(2 * t + q).wait()
            for f in range(2):
                for r in range(N):
                    v = xm[2 + f, (2 * t + q) * N + 1 + r].astype(F32)
                    i = (2 * q + f) * N + r
                    ends[0, i : i + 1] = v[WD - 1:]
                    ends[1, i : i + 1] = v[:1]
        for side in (0, 1):
            cs[side, t] = ends[side].astype(BF16)
        return carry

    lax.fori_loop(0, PAIRS, own_columns, 0)

    pl.semaphore_wait(barrier, len(far + near) + jnp.where((z == 0) | (z == 7), 1, 0))

    def remote(src, dst, s, r, dev):
        return pltpu.make_async_remote_copy(
            src_ref=src, dst_ref=dst, send_sem=s, recv_sem=r, device_id=dev, device_id_type=MESH)

    def main(c, row):
        return remote(
            x_ref.at[:, pl.ds(row, N)], xm.at[pl.ds(0, 2), pl.ds(row + 1, N)],
            main_s.at[c], main_r.at[c], partner)

    def last(half):
        row = chunk_row(CHUNKS - 1) + half * N // 2
        return remote(
            x_ref.at[:, pl.ds(row, N // 2)], xm.at[pl.ds(0, 2), pl.ds(row + 1, N // 2)],
            main_s.at[CHUNKS - 1 + half], main_r.at[CHUNKS - 1 + half], partner)

    def own_strip(side):
        return remote(cs.at[side], ph.at[1, side], own_s.at[side], own_r.at[side], (tm, lat, (right, left)[side]))

    def pack_strip():
        return remote(ph.at[1], ph.at[0], pack_s.at[0], pack_r.at[0], partner)

    def back_strip():
        span = pl.ds(BACK_ROW // (2 * N), (BACK_ROW + BACK * N - 1) // (2 * N) - BACK_ROW // (2 * N) + 1)
        return remote(ph.at[1, :, span], ph.at[0, :, span], back_s.at[0], back_r.at[0], partner)

    def unpack(k, pairs):
        for t in pairs:
            for side in (0, 1):
                v = ph[k, side, t].astype(F32)
                ch[k, 2 * t, side] = v[: 2 * N]
                ch[k, 2 * t + 1, side] = v[2 * N :]

    def rows(k, way, part):
        la = (lat + 1) % 4 if way == 0 else (lat + 3) % 4
        sems = (row_s.at[k, way, part], row_r.at[k, way, part], (tm, la, lon))
        if part:
            return remote(ch.at[k, 0 if way == 1 else CHUNKS - 1], cc.at[k, way], *sems)
        p = H if way == 0 else 1
        q = 0 if way == 0 else H + 1
        base = x_ref.at[:, pl.ds(p - 1, 1)] if k else xm.at[pl.ds(0, 2), pl.ds(p, 1)]
        return remote(base, xm.at[pl.ds(2 * k, 2), pl.ds(q, 1)], *sems)

    def rows_start(k, way, part):
        @pl.when(has_dn if way == 0 else has_up)
        def _():
            rows(k, way, part).start()

    for side in (0, 1):
        own_strip(side).start()

    @pl.when(first)
    def _():
        for c in range(EARLY):
            main(c, chunk_row(c)).start()

    for way in (0, 1):
        rows_start(1, way, 0)

    @pl.when(second)
    def _():
        for c in range(2):
            main(c, BACK_ROW + c * N).start()

    for cp in params:
        cp.wait()

    def shifted(slot, p, ends, row):
        col = lax.broadcasted_iota(jnp.int32, (WD, C), 0)
        for f in range(2):
            v = xm[slot + f, p].astype(F32)
            i = f * N + row
            a, b = ends[0, i : i + 1], ends[1, i : i + 1]
            xl[slot + f, p] = jnp.where(col == 0, a, pltpu.roll(v, 1, 0)).astype(BF16)
            xr[slot + f, p] = jnp.where(col == WD - 1, b, pltpu.roll(v, WD - 1, 0)).astype(BF16)

    def taps(slot, p, n):
        return [v[slot, pl.ds(p, n)].reshape(n * WD, C) for v in (xl, xm, xr)]

    def own_planes(slot, h, n, off, add):
        ahead = [jnp.concatenate([v for b in range(3) for v in taps(slot + f, h + b, n)], axis=1) for f in range(2)]
        y = jnp.dot(ahead[0], wt[:, :, : 2 * C].reshape(9 * C, 2 * C), preferred_element_type=F32)
        z = jnp.dot(ahead[1], wt[:, :, :C].reshape(9 * C, C), preferred_element_type=F32)
        rr = pl.ds(h + 1 + off, n)
        if add:
            acc[0, rr] += y[:, :C].reshape(n, WD, C)
            acc[1, rr] += (y[:, C:] + z).reshape(n, WD, C)
        else:
            bias = bias_ref[...].reshape(1, C)
            acc[0, rr] = (y[:, :C] + bias).reshape(n, WD, C)
            acc[1, rr] = (y[:, C:] + z + bias).reshape(n, WD, C)

    def prev_planes(slot, p, n, off, rows_b=(0, 1, 2)):
        older = jnp.concatenate(taps(slot, p, n), axis=1)
        newer = jnp.concatenate(taps(slot + 1, p, n), axis=1)
        for b in rows_b:
            rr = pl.ds(p + 1 - b + off, n)
            z = jnp.dot(older, wt[b, :, 2 * C :], preferred_element_type=F32)
            y = jnp.dot(newer, wt[b, :, C:], preferred_element_type=F32)
            acc[0, rr] += (y[:, :C] + z).reshape(n, WD, C)
            acc[1, rr] += y[:, C:].reshape(n, WD, C)

    def prev_block(slot, h, n, off):
        ahead = [jnp.concatenate([v for b in range(3) for v in taps(slot + f, h + b, n)], axis=1) for f in range(2)]
        z = jnp.dot(ahead[0], wt[:, :, 2 * C :].reshape(9 * C, C), preferred_element_type=F32)
        y = jnp.dot(ahead[1], wt[:, :, C:].reshape(9 * C, 2 * C), preferred_element_type=F32)
        bias = bias_ref[...].reshape(1, C)
        rr = pl.ds(h + 1 + off, n)
        acc[0, rr] = (y[:, :C] + z + bias).reshape(n, WD, C)
        acc[1, rr] = (y[:, C:] + bias).reshape(n, WD, C)

    def edge_rows(k):
        for way in (0, 1):
            ok = has_up if way == 0 else has_dn
            p = 0 if way == 0 else H + 1

            @pl.when(ok)
            def _():
                for part in (0, 1):
                    rows(k, way, part).wait_recv()
                shifted(2 * k, p, cc.at[k, way], N - 1 if way == 0 else 0)
                if k == 0:
                    prev_planes(0, p, 1, 0, (0,) if way == 0 else (2,))

            if k:
                @pl.when(jnp.logical_not(ok))
                def _():
                    for v in (xl, xm, xr):
                        v[pl.ds(2, 2), pl.ds(p, 1)] = jnp.zeros((2, 1, WD, C), BF16)

    def other_p(c):
        return jnp.where(first, BACK_ROW + 1 + c * N, chunk_row(c) + 1)

    for side in (0, 1):
        own_strip(side).wait_recv()

    @pl.when(second)
    def _():
        back_strip().start()
        for c in range(2, BACK):
            main(c, BACK_ROW + c * N).start()

    @pl.when(first)
    def _():
        pack_strip().start()
        for c in range(EARLY, CHUNKS - 1):
            main(c, chunk_row(c)).start()
        last(0).start()

    unpack(1, range(PAIRS))
    for way in (0, 1):
        rows_start(1, way, 1)

    def own_shift(q):
        for r in range(N):
            shifted(2, 1 + q * N + r, ch.at[1, q], r)

    for q in range(1, 5):
        own_shift(q)
    load_w(2).wait()
    load_w(1).wait()
    blocks = H // BLOCK

    def own_step(i, carry):
        @pl.when(i == blocks - 2)
        def _():
            edge_rows(1)

        own_planes(2, (i + 1) % blocks * BLOCK, BLOCK, 0, False)
        for k in (5, 6):
            own_shift((2 * i + k) % CHUNKS)
        return carry

    lax.fori_loop(0, blocks, own_step, 0)
    load_w(0).wait()

    count = jnp.where(first, float(H + SHARED), float(H - SHARED)) * (2 * WD * PER)
    other_count = jnp.where(first, float(H - SHARED), float(H + SHARED)) * (2 * WD * PER)
    sub = lax.broadcasted_iota(jnp.int32, (8, 128), 0)

    def pack(mean, m2):
        return jnp.where(sub == 0, mean, jnp.where(sub == 1, m2, 0.0))

    def over_rows():
        pivot = aff[8:16]

        def step(r, sums):
            d = acc[:, r].reshape(2 * WD // 8, 8, C) - pivot
            return sums[0] + d.sum(0), sums[1] + (d * d).sum(0)

        sums = (jnp.zeros((8, C), F32), jnp.zeros((8, C), F32))
        sums = lax.fori_loop(1, jnp.where(first, 1 + H, 1 + SHARE_LO), step, sums)
        sums = lax.fori_loop(
            jnp.where(first, 1 + SHARE_LO + OFF, 1 + SHARE_HI), jnp.where(first, 1 + SHARE_HI + OFF, 1 + H), step, sums)
        return [jnp.broadcast_to(v.sum(0, keepdims=True), (8, C)) for v in sums]

    def group(v):
        return jnp.dot(v, g_in[...], precision=HIGH, preferred_element_type=F32)

    def channel(v):
        return jnp.dot(v, g_out[...], precision=HIGH, preferred_element_type=F32)

    def r1_copy(i):
        return remote(r1.at[0], r1.at[i + 1], r1_s.at[i], r1_r.at[i], near[i])

    def r2_copy(i):
        return remote(r2.at[0], r2.at[i + 1], r2_s.at[i], r2_r.at[i], far[i])

    def stats_pivot():
        v = acc[:, PIVOT].reshape(2 * WD // 8, 8, C).sum(0).sum(0, keepdims=True)
        mean = group(jnp.broadcast_to(v, (8, C))) * (1.0 / (2 * WD * PER))
        stat[...] = mean
        aff[8:16] = channel(mean)

    def stats_begin():
        s1, s2 = over_rows()
        sums = group(jnp.where(lax.broadcasted_iota(jnp.int32, (8, C), 0) == 0, s1, s2))
        shift = sums[0:1] / count
        m2 = jnp.maximum(sums[1:2] - sums[0:1] * shift, 0.0)
        r1[0] = pack(stat[...] + shift, jnp.broadcast_to(m2, (8, 128)))
        for i in range(7):
            r1_copy(i).start()

    def stats_middle():
        for i in range(7):
            r1_copy(i).wait_recv()
        means = [r1[i, 0:1] for i in range(8)]
        mean = sum(means) * 0.125
        m2 = sum(r1[i, 1:2] for i in range(8)) + count * sum((m - mean) * (m - mean) for m in means)
        r2[0] = pack(jnp.broadcast_to(mean, (8, 128)), jnp.broadcast_to(m2, (8, 128)))
        for i in range(15):
            r2_copy(i).start()

    def stats_end():
        for i in range(15):
            r2_copy(i).wait_recv()
        means = [r2[i, 0:1] for i in range(16)]
        mine, other = 8.0 * count, 8.0 * other_count
        total = 8.0 * (mine + other)
        mean = (mine * sum(means[:8]) + other * sum(means[8:])) / total
        m2 = sum(r2[i, 1:2] for i in range(16))
        m2 = m2 + mine * sum((m - mean) * (m - mean) for m in means[:8])
        m2 = m2 + other * sum((m - mean) * (m - mean) for m in means[8:])
        inv = lax.rsqrt(m2 / total + 1e-6)
        both = channel(pack(jnp.broadcast_to(mean, (8, 128)), jnp.broadcast_to(inv, (8, 128))))
        aff[0:1] = both[0:1]
        aff[1:2] = both[1:2] * gain_ref[...].reshape(1, C)

    def finish(lo, hi, skip=0):
        mean, scale, shift = aff[0:1], aff[1:2], shift_ref[...].reshape(1, C)

        def step(i, carry):
            r = i + jnp.where(i >= END_LO, skip, 0)
            v = acc[:, r + 1].reshape(2 * WD, C)
            v = (v - mean) * scale + shift
            v = v / (1.0 + jnp.exp(-v))
            o_ref[:, r] = v.astype(BF16).reshape(2, WD, C)
            return carry

        lax.fori_loop(lo, hi, step, 0)

    @pl.when(second)
    def _():
        pack_strip().wait_recv()
        unpack(0, range(PAIRS))
        for way in (0, 1):
            rows_start(0, way, 1)

    def drain():
        for i in range(7):
            r1_copy(i).wait_send()
        for i in range(15):
            r2_copy(i).wait_send()
        for side in (0, 1):
            own_strip(side).wait_send()

        def sent(c, carry):
            main(c, c * N).wait_send()
            return carry

        lax.fori_loop(0, jnp.where(first, CHUNKS - 1, BACK), sent, 0)

        @pl.when(first)
        def _():
            pack_strip().wait_send()
            for half in (0, 1):
                last(half).wait_send()

        @pl.when(second)
        def _():
            back_strip().wait_send()

        for k in (1, 0):
            for way in (0, 1):
                ok = has_dn if way == 0 else has_up

                @pl.when(ok if k else ok & second)
                def _():
                    for part in (0, 1):
                        rows(k, way, part).wait_send()

    whole = 5

    def prev_step(c, carry):
        row = chunk_row(c)
        p = row + 1

        @pl.when(c < CHUNKS - 1)
        def _():
            main(c, row).wait_recv()

        @pl.when(c == CHUNKS - 1)
        def _():
            for half in (0, 1):
                last(half).wait_recv()


        @pl.when(c == 0)
        def _():
            rows_start(0, 1, 0)

        @pl.when(c == 1)
        def _():
            rows_start(0, 0, 0)

        @pl.when(c == whole - 1)
        def _():
            edge_rows(0)
            stats_pivot()

        for r in range(N):
            shifted(0, p + r, ch.at[0, row // N], r)
        prev_planes(0, p, N, 0)

        @pl.when(c == whole)
        def _():
            stats_begin()

        @pl.when(c == whole + 1)
        def _():
            stats_middle()

        @pl.when(c == CHUNKS - 2)
        def _():
            stats_end()
            drain()

        @pl.when(c >= CHUNKS - 2)
        def _():
            early = c == CHUNKS - 2
            gap = END_HI - END_LO
            finish(jnp.where(early, 0, END_LO), jnp.where(early, H - gap, END_HI), jnp.where(early, gap, 0))

        return carry

    @pl.when(second)
    def _():
        lax.fori_loop(0, CHUNKS, prev_step, 0)

    @pl.when(first)
    def _():
        def shared_prev(i, carry):
            prev_block(2, BACK_ROW + i * SHARE_BLOCK, SHARE_BLOCK, OFF)
            return carry

        lax.fori_loop(0, BACK * N // SHARE_BLOCK, shared_prev, 0)
        stats_pivot()
        back_strip().wait_recv()
        unpack(0, range(BACK_ROW // (2 * N), (BACK_ROW + BACK * N - 1) // (2 * N) + 1))
        for j in range(BACK):
            p = BACK_ROW + 1 + j * N
            main(j, p - 1).wait_recv()
            for r in range(N):
                shifted(0, p + r, ch.at[0, BACK_ROW // N + j + (SKEW + r) // N], (SKEW + r) % N)

        def shared_step(i, carry):
            own_planes(0, BACK_ROW + i * SHARE_BLOCK, SHARE_BLOCK, OFF, True)
            return carry

        lax.fori_loop(0, BACK * N // SHARE_BLOCK, shared_step, 0)
        stats_begin()
        stats_middle()
        last(1).start()
        stats_end()
        finish(0, H)
        drain()

def body(latents, conv_weight, conv_bias, norm_gain, norm_shift):
    vmem = pl.BlockSpec(memory_space=pltpu.VMEM)
    hbm = pl.BlockSpec(memory_space=pltpu.HBM)
    dma = pltpu.SemaphoreType.DMA
    halo = pltpu.VMEM((4, H + 2, WD, C), BF16)
    packed = (2, PAIRS, 4 * N, C)
    return pl.pallas_call(
        kernel,
        out_shape=pltpu.VMEM(latents.shape, BF16),
        in_specs=[hbm] * 5,
        out_specs=vmem,
        scratch_shapes=[
            pltpu.VMEM((C,), F32), pltpu.VMEM((C,), F32), pltpu.VMEM((C,), F32),
            pltpu.VMEM((3, 3 * C, 3 * C), BF16), halo, halo, halo,
            pltpu.VMEM((2, 4 * N, C), F32), pltpu.VMEM(packed, BF16), pltpu.VMEM((2,) + packed, BF16),
            pltpu.VMEM((2, CHUNKS, 2, 2 * N, C), F32), pltpu.VMEM((2, 2, 2, 2 * N, C), F32),
            pltpu.VMEM((2, ACC_ROWS, WD, C), F32),
            pltpu.VMEM((C, 128), F32), pltpu.VMEM((128, C), F32),
            pltpu.VMEM((16, C), F32), pltpu.VMEM((8, 128), F32),
            pltpu.VMEM((8, 8, 128), F32), pltpu.VMEM((16, 8, 128), F32),
            dma((CHUNKS,)), dma((3,)), dma((3,)), dma((CHUNKS + 1,)), dma((CHUNKS + 1,)),
            dma((2,)), dma((2,)), dma((1,)), dma((1,)), dma((1,)), dma((1,)),
            dma((2, 2, 2)), dma((2, 2, 2)),
            dma((7,)), dma((7,)), dma((15,)), dma((15,)),
        ],
        compiler_params=pltpu.CompilerParams(
            collective_id=0, has_side_effects=True, vmem_limit_bytes=48 * 2**20),
        cost_estimate=pl.CostEstimate(flops=20 * 10**9, bytes_accessed=16 * 2**20, transcendentals=10**6),
        name="conv_norm_silu",
    )(
        *(pltpu.with_memory_space_constraint(v, pltpu.HBM) for v in (
            latents, conv_weight.reshape(3, 3, 3 * C, C), conv_bias, norm_gain, norm_shift)))


def solution(mesh):
    spec = P("tm", "lat", "lon", None)
    return jax.shard_map(
        body, mesh=mesh, in_specs=(spec, P(), P(), P(), P()), out_specs=spec, check_vma=False)
```

```python
import functools

import jax
import jax.numpy as jnp
from jax import lax
from jax.experimental import pallas as pl
from jax.experimental.pallas import tpu as pltpu
from jax.sharding import PartitionSpec as P

MESH = pl.DeviceIdType.MESH
F32, BF16 = jnp.float32, jnp.bfloat16
HIGH = lax.Precision.HIGHEST

GROUPS = 32
C = 384
PER = C // GROUPS
H, WD = 40, 32
N = 4
CHUNKS = H // N

SHARE_LO, SHARE_HI = 11, 29
BACK = (SHARE_HI - SHARE_LO + 2) // N
BACK_ROW = SHARE_LO - 1
OFF = 33
ACC_ROWS = 64
BLOCK = 8
SHARE_BLOCK = 10
SHARED = SHARE_HI - SHARE_LO
EARLY = 3
SKEW = BACK_ROW % N
PAIRS = CHUNKS // 2
END_LO, END_HI = 19, 25
PIVOT = 6


def chunk_row(c):
    odd = c % 2
    half = c // 2
    return N * ((1 - odd) * half + odd * (CHUNKS - 1 - half))


def kernel(
    x_ref, w_ref, bias_in, gain_in, shift_in, o_ref,
    bias_ref, gain_ref, shift_ref,    wt, xm, xl, xr, ends, cs, ph, ch, cc, acc, g_in, g_out, aff, stat, r1, r2,
    loc_sem, w_sem, par_sem, main_s, main_r, own_s, own_r, pack_s, pack_r, back_s, back_r, row_s, row_r, r1_s, r1_r, r2_s, r2_r,
):
    tm, lat, lon = (lax.axis_index(a) for a in ("tm", "lat", "lon"))
    left, right = (lon + 15) % 16, (lon + 1) % 16
    z, yl = lon % 8, lon // 8
    first, second = tm == 0, tm == 1
    has_up, has_dn = lat > 0, lat < 3
    partner = (1 - tm, lat, lon)
    near = [(tm, lat, yl * 8 + (z + d) % 8) for d in range(1, 8)]
    far = [
        ((tm + a) % 2, (lat + b) % 4, ((yl + c) % 2) * 8 + z)
        for a in range(2) for b in range(4) for c in range(2)
    ][1:]

    barrier = pltpu.get_barrier_semaphore()
    for peer in far + near:
        pl.semaphore_signal(barrier, inc=1, device_id=peer, device_id_type=MESH)

    @pl.when(z == 7)
    def _():
        pl.semaphore_signal(barrier, inc=1, device_id=(tm, lat, right), device_id_type=MESH)

    @pl.when(z == 0)
    def _():
        pl.semaphore_signal(barrier, inc=1, device_id=(tm, lat, left), device_id_type=MESH)

    def load_x(c):
        return pltpu.make_async_copy(
            x_ref.at[:, pl.ds(c * N, N)], xm.at[pl.ds(2, 2), pl.ds(c * N + 1, N)], loc_sem.at[c])

    def load_w(a):
        return pltpu.make_async_copy(w_ref.at[a], wt.at[:, :, pl.ds((2 - a) * C, C)], w_sem.at[a])

    params = [
        pltpu.make_async_copy(src, dst, par_sem.at[i])
        for i, (src, dst) in enumerate(((bias_in, bias_ref), (gain_in, gain_ref), (shift_in, shift_ref)))]
    for cp in params:
        cp.start()
    for c in range(CHUNKS):
        load_x(c).start()
    for a in (2, 1, 0):
        load_w(a).start()

    row_i = lax.broadcasted_iota(jnp.int32, (C, 128), 0)
    lane_i = lax.broadcasted_iota(jnp.int32, (C, 128), 1)
    delta = row_i - PER * lane_i
    g_in[...] = jnp.where((delta >= 0) & (delta < PER), 1.0, 0.0)
    row_i = lax.broadcasted_iota(jnp.int32, (128, C), 0)
    lane_i = lax.broadcasted_iota(jnp.int32, (128, C), 1)
    delta = lane_i - PER * row_i
    g_out[...] = jnp.where((delta >= 0) & (delta < PER), 1.0, 0.0)

    def own_columns(t, carry):
        for q in range(2):
            load_x(2 * t + q).wait()
            for f in range(2):
                for r in range(N):
                    v = xm[2 + f, (2 * t + q) * N + 1 + r].astype(F32)
                    i = (2 * q + f) * N + r
                    ends[0, i : i + 1] = v[WD - 1:]
                    ends[1, i : i + 1] = v[:1]
        for side in (0, 1):
            cs[side, t] = ends[side].astype(BF16)
        return carry

    lax.fori_loop(0, PAIRS, own_columns, 0)

    pl.semaphore_wait(barrier, len(far + near) + jnp.where((z == 0) | (z == 7), 1, 0))

    def remote(src, dst, s, r, dev):
        return pltpu.make_async_remote_copy(
            src_ref=src, dst_ref=dst, send_sem=s, recv_sem=r, device_id=dev, device_id_type=MESH)

    def main(c, row):
        return remote(
            x_ref.at[:, pl.ds(row, N)], xm.at[pl.ds(0, 2), pl.ds(row + 1, N)],
            main_s.at[c], main_r.at[c], partner)

    def last(half):
        row = chunk_row(CHUNKS - 1) + half
        n = N - 1 if half else 1
        return remote(
            x_ref.at[:, pl.ds(row, n)], xm.at[pl.ds(0, 2), pl.ds(row + 1, n)],
            main_s.at[CHUNKS - 1 + half], main_r.at[CHUNKS - 1 + half], partner)

    def own_strip(side):
        return remote(cs.at[side], ph.at[1, side], own_s.at[side], own_r.at[side], (tm, lat, (right, left)[side]))

    def pack_strip():
        return remote(ph.at[1], ph.at[0], pack_s.at[0], pack_r.at[0], partner)

    def back_strip():
        span = pl.ds(BACK_ROW // (2 * N), (BACK_ROW + BACK * N - 1) // (2 * N) - BACK_ROW // (2 * N) + 1)
        return remote(ph.at[1, :, span], ph.at[0, :, span], back_s.at[0], back_r.at[0], partner)

    def unpack(k, pairs):
        for t in pairs:
            for side in (0, 1):
                v = ph[k, side, t].astype(F32)
                ch[k, 2 * t, side] = v[: 2 * N]
                ch[k, 2 * t + 1, side] = v[2 * N :]

    def rows(k, way, part):
        la = (lat + 1) % 4 if way == 0 else (lat + 3) % 4
        sems = (row_s.at[k, way, part], row_r.at[k, way, part], (tm, la, lon))
        if part:
            return remote(ch.at[k, 0 if way == 1 else CHUNKS - 1], cc.at[k, way], *sems)
        p = H if way == 0 else 1
        q = 0 if way == 0 else H + 1
        base = x_ref.at[:, pl.ds(p - 1, 1)] if k else xm.at[pl.ds(0, 2), pl.ds(p, 1)]
        return remote(base, xm.at[pl.ds(2 * k, 2), pl.ds(q, 1)], *sems)

    def rows_start(k, way, part):
        @pl.when(has_dn if way == 0 else has_up)
        def _():
            rows(k, way, part).start()

    for side in (0, 1):
        own_strip(side).start()

    @pl.when(first)
    def _():
        for c in range(EARLY):
            main(c, chunk_row(c)).start()

    for way in (0, 1):
        rows_start(1, way, 0)

    @pl.when(second)
    def _():
        for c in range(2):
            main(c, BACK_ROW + c * N).start()

    for cp in params:
        cp.wait()

    def shifted(slot, p, ends, row):
        col = lax.broadcasted_iota(jnp.int32, (WD, C), 0)
        for f in range(2):
            v = xm[slot + f, p].astype(F32)
            i = f * N + row
            a, b = ends[0, i : i + 1], ends[1, i : i + 1]
            xl[slot + f, p] = jnp.where(col == 0, a, pltpu.roll(v, 1, 0)).astype(BF16)
            xr[slot + f, p] = jnp.where(col == WD - 1, b, pltpu.roll(v, WD - 1, 0)).astype(BF16)

    def taps(slot, p, n):
        return [v[slot, pl.ds(p, n)].reshape(n * WD, C) for v in (xl, xm, xr)]

    def own_planes(slot, h, n, off, add):
        ahead = [jnp.concatenate([v for b in range(3) for v in taps(slot + f, h + b, n)], axis=1) for f in range(2)]
        y = jnp.dot(ahead[0], wt[:, :, : 2 * C].reshape(9 * C, 2 * C), preferred_element_type=F32)
        z = jnp.dot(ahead[1], wt[:, :, :C].reshape(9 * C, C), preferred_element_type=F32)
        rr = pl.ds(h + 1 + off, n)
        if add:
            acc[0, rr] += y[:, :C].reshape(n, WD, C)
            acc[1, rr] += (y[:, C:] + z).reshape(n, WD, C)
        else:
            bias = bias_ref[...].reshape(1, C)
            acc[0, rr] = (y[:, :C] + bias).reshape(n, WD, C)
            acc[1, rr] = (y[:, C:] + z + bias).reshape(n, WD, C)

    def prev_planes(slot, p, n, off, rows_b=(0, 1, 2)):
        older = jnp.concatenate(taps(slot, p, n), axis=1)
        newer = jnp.concatenate(taps(slot + 1, p, n), axis=1)
        for b in rows_b:
            rr = pl.ds(p + 1 - b + off, n)
            z = jnp.dot(older, wt[b, :, 2 * C :], preferred_element_type=F32)
            y = jnp.dot(newer, wt[b, :, C:], preferred_element_type=F32)
            acc[0, rr] += (y[:, :C] + z).reshape(n, WD, C)
            acc[1, rr] += y[:, C:].reshape(n, WD, C)

    def prev_block(slot, h, n, off):
        ahead = [jnp.concatenate([v for b in range(3) for v in taps(slot + f, h + b, n)], axis=1) for f in range(2)]
        z = jnp.dot(ahead[0], wt[:, :, 2 * C :].reshape(9 * C, C), preferred_element_type=F32)
        y = jnp.dot(ahead[1], wt[:, :, C:].reshape(9 * C, 2 * C), preferred_element_type=F32)
        bias = bias_ref[...].reshape(1, C)
        rr = pl.ds(h + 1 + off, n)
        acc[0, rr] = (y[:, :C] + z + bias).reshape(n, WD, C)
        acc[1, rr] = (y[:, C:] + bias).reshape(n, WD, C)

    def edge_rows(k):
        for way in (0, 1):
            ok = has_up if way == 0 else has_dn
            p = 0 if way == 0 else H + 1

            @pl.when(ok)
            def _():
                for part in (0, 1):
                    rows(k, way, part).wait_recv()
                shifted(2 * k, p, cc.at[k, way], N - 1 if way == 0 else 0)
                if k == 0:
                    prev_planes(0, p, 1, 0, (0,) if way == 0 else (2,))

            if k:
                @pl.when(jnp.logical_not(ok))
                def _():
                    for v in (xl, xm, xr):
                        v[pl.ds(2, 2), pl.ds(p, 1)] = jnp.zeros((2, 1, WD, C), BF16)

    def other_p(c):
        return jnp.where(first, BACK_ROW + 1 + c * N, chunk_row(c) + 1)

    for side in (0, 1):
        own_strip(side).wait_recv()

    @pl.when(second)
    def _():
        back_strip().start()
        for c in range(2, BACK):
            main(c, BACK_ROW + c * N).start()

    @pl.when(first)
    def _():
        pack_strip().start()
        for c in range(EARLY, CHUNKS - 1):
            main(c, chunk_row(c)).start()
        last(0).start()

    unpack(1, range(PAIRS))
    for way in (0, 1):
        rows_start(1, way, 1)

    def own_shift(q):
        for r in range(N):
            shifted(2, 1 + q * N + r, ch.at[1, q], r)

    for q in range(1, 5):
        own_shift(q)
    load_w(2).wait()
    load_w(1).wait()
    blocks = H // BLOCK

    def own_step(i, carry):
        @pl.when(i == blocks - 2)
        def _():
            edge_rows(1)

        own_planes(2, (i + 1) % blocks * BLOCK, BLOCK, 0, False)
        for k in (5, 6):
            own_shift((2 * i + k) % CHUNKS)
        return carry

    lax.fori_loop(0, blocks, own_step, 0)
    load_w(0).wait()

    count = jnp.where(first, float(H + SHARED), float(H - SHARED)) * (2 * WD * PER)
    other_count = jnp.where(first, float(H - SHARED), float(H + SHARED)) * (2 * WD * PER)
    sub = lax.broadcasted_iota(jnp.int32, (8, 128), 0)

    def pack(mean, m2):
        return jnp.where(sub == 0, mean, jnp.where(sub == 1, m2, 0.0))

    def over_rows():
        pivot = aff[8:16]

        def step(r, sums):
            d = acc[:, r].reshape(2 * WD // 8, 8, C) - pivot
            return sums[0] + d.sum(0), sums[1] + (d * d).sum(0)

        sums = (jnp.zeros((8, C), F32), jnp.zeros((8, C), F32))
        sums = lax.fori_loop(1, jnp.where(first, 1 + H, 1 + SHARE_LO), step, sums)
        sums = lax.fori_loop(
            jnp.where(first, 1 + SHARE_LO + OFF, 1 + SHARE_HI), jnp.where(first, 1 + SHARE_HI + OFF, 1 + H), step, sums)
        return [jnp.broadcast_to(v.sum(0, keepdims=True), (8, C)) for v in sums]

    def group(v):
        return jnp.dot(v, g_in[...], precision=HIGH, preferred_element_type=F32)

    def channel(v):
        return jnp.dot(v, g_out[...], precision=HIGH, preferred_element_type=F32)

    def r1_copy(i):
        return remote(r1.at[0], r1.at[i + 1], r1_s.at[i], r1_r.at[i], near[i])

    def r2_copy(i):
        return remote(r2.at[0], r2.at[i + 1], r2_s.at[i], r2_r.at[i], far[i])

    def stats_pivot():
        v = acc[:, PIVOT].reshape(2 * WD // 8, 8, C).sum(0).sum(0, keepdims=True)
        mean = group(jnp.broadcast_to(v, (8, C))) * (1.0 / (2 * WD * PER))
        stat[...] = mean
        aff[8:16] = channel(mean)

    def stats_begin():
        s1, s2 = over_rows()
        sums = group(jnp.where(lax.broadcasted_iota(jnp.int32, (8, C), 0) == 0, s1, s2))
        shift = sums[0:1] / count
        m2 = jnp.maximum(sums[1:2] - sums[0:1] * shift, 0.0)
        r1[0] = pack(stat[...] + shift, jnp.broadcast_to(m2, (8, 128)))
        for i in range(7):
            r1_copy(i).start()

    def stats_middle(order):
        for i in range(7):
            r1_copy(i).wait_recv()
        means = [r1[i, 0:1] for i in range(8)]
        mean = sum(means) * 0.125
        m2 = sum(r1[i, 1:2] for i in range(8)) + count * sum((m - mean) * (m - mean) for m in means)
        r2[0] = pack(jnp.broadcast_to(mean, (8, 128)), jnp.broadcast_to(m2, (8, 128)))
        for i in order:
            r2_copy(i).start()

    def stats_end():
        for i in range(15):
            r2_copy(i).wait_recv()
        means = [r2[i, 0:1] for i in range(16)]
        mine, other = 8.0 * count, 8.0 * other_count
        total = 8.0 * (mine + other)
        mean = (mine * sum(means[:8]) + other * sum(means[8:])) / total
        m2 = sum(r2[i, 1:2] for i in range(16))
        m2 = m2 + mine * sum((m - mean) * (m - mean) for m in means[:8])
        m2 = m2 + other * sum((m - mean) * (m - mean) for m in means[8:])
        inv = lax.rsqrt(m2 / total + 1e-6)
        both = channel(pack(jnp.broadcast_to(mean, (8, 128)), jnp.broadcast_to(inv, (8, 128))))
        aff[0:1] = both[0:1]
        aff[1:2] = both[1:2] * gain_ref[...].reshape(1, C)

    def finish(lo, hi, skip=0):
        mean, scale, shift = aff[0:1], aff[1:2], shift_ref[...].reshape(1, C)

        def step(i, carry):
            r = i + jnp.where(i >= END_LO, skip, 0)
            v = acc[:, r + 1].reshape(2 * WD, C)
            v = (v - mean) * scale + shift
            v = v / (1.0 + jnp.exp(-v))
            o_ref[:, r] = v.astype(BF16).reshape(2, WD, C)
            return carry

        lax.fori_loop(lo, hi, step, 0)

    @pl.when(second)
    def _():
        pack_strip().wait_recv()
        unpack(0, range(PAIRS))
        for way in (0, 1):
            rows_start(0, way, 1)

    def drain():
        for i in range(7):
            r1_copy(i).wait_send()
        for i in range(15):
            r2_copy(i).wait_send()
        for side in (0, 1):
            own_strip(side).wait_send()

        def sent(c, carry):
            main(c, c * N).wait_send()
            return carry

        lax.fori_loop(0, jnp.where(first, CHUNKS - 1, BACK), sent, 0)

        @pl.when(first)
        def _():
            pack_strip().wait_send()
            for half in (0, 1):
                last(half).wait_send()

        @pl.when(second)
        def _():
            back_strip().wait_send()

        for k in (1, 0):
            for way in (0, 1):
                ok = has_dn if way == 0 else has_up

                @pl.when(ok if k else ok & second)
                def _():
                    for part in (0, 1):
                        rows(k, way, part).wait_send()

    whole = 5

    def prev_step(c, carry):
        row = chunk_row(c)
        p = row + 1

        @pl.when(c < CHUNKS - 1)
        def _():
            main(c, row).wait_recv()

        @pl.when(c == CHUNKS - 1)
        def _():
            for half in (0, 1):
                last(half).wait_recv()


        @pl.when(c == 0)
        def _():
            rows_start(0, 1, 0)

        @pl.when(c == 1)
        def _():
            rows_start(0, 0, 0)

        @pl.when(c == whole - 1)
        def _():
            edge_rows(0)
            stats_pivot()

        for r in range(N):
            shifted(0, p + r, ch.at[0, row // N], r)
        prev_planes(0, p, N, 0)

        @pl.when(c == whole)
        def _():
            stats_begin()

        @pl.when(c == whole + 1)
        def _():
            stats_middle(range(15))

        @pl.when(c == CHUNKS - 2)
        def _():
            stats_end()
            drain()

        @pl.when(c >= CHUNKS - 2)
        def _():
            early = c == CHUNKS - 2
            gap = END_HI - END_LO
            finish(jnp.where(early, 0, END_LO), jnp.where(early, H - gap, END_HI), jnp.where(early, gap, 0))

        return carry

    @pl.when(second)
    def _():
        lax.fori_loop(0, CHUNKS, prev_step, 0)

    @pl.when(first)
    def _():
        def shared_prev(i, carry):
            prev_block(2, BACK_ROW + i * SHARE_BLOCK, SHARE_BLOCK, OFF)
            return carry

        lax.fori_loop(0, BACK * N // SHARE_BLOCK, shared_prev, 0)
        stats_pivot()
        back_strip().wait_recv()
        unpack(0, range(BACK_ROW // (2 * N), (BACK_ROW + BACK * N - 1) // (2 * N) + 1))
        for j in range(BACK):
            p = BACK_ROW + 1 + j * N
            main(j, p - 1).wait_recv()
            for r in range(N):
                shifted(0, p + r, ch.at[0, BACK_ROW // N + j + (SKEW + r) // N], (SKEW + r) % N)

        def shared_step(i, carry):
            own_planes(0, BACK_ROW + i * SHARE_BLOCK, SHARE_BLOCK, OFF, True)
            return carry

        lax.fori_loop(0, BACK * N // SHARE_BLOCK, shared_step, 0)
        stats_begin()
        stats_middle(range(14, -1, -1))
        last(1).start()
        stats_end()
        finish(0, H)
        drain()

def body(latents, conv_weight, conv_bias, norm_gain, norm_shift):
    vmem = pl.BlockSpec(memory_space=pltpu.VMEM)
    hbm = pl.BlockSpec(memory_space=pltpu.HBM)
    dma = pltpu.SemaphoreType.DMA
    halo = pltpu.VMEM((4, H + 2, WD, C), BF16)
    packed = (2, PAIRS, 4 * N, C)
    return pl.pallas_call(
        kernel,
        out_shape=pltpu.VMEM(latents.shape, BF16),
        in_specs=[hbm] * 5,
        out_specs=vmem,
        scratch_shapes=[
            pltpu.VMEM((C,), F32), pltpu.VMEM((C,), F32), pltpu.VMEM((C,), F32),
            pltpu.VMEM((3, 3 * C, 3 * C), BF16), halo, halo, halo,
            pltpu.VMEM((2, 4 * N, C), F32), pltpu.VMEM(packed, BF16), pltpu.VMEM((2,) + packed, BF16),
            pltpu.VMEM((2, CHUNKS, 2, 2 * N, C), F32), pltpu.VMEM((2, 2, 2, 2 * N, C), F32),
            pltpu.VMEM((2, ACC_ROWS, WD, C), F32),
            pltpu.VMEM((C, 128), F32), pltpu.VMEM((128, C), F32),
            pltpu.VMEM((16, C), F32), pltpu.VMEM((8, 128), F32),
            pltpu.VMEM((8, 8, 128), F32), pltpu.VMEM((16, 8, 128), F32),
            dma((CHUNKS,)), dma((3,)), dma((3,)), dma((CHUNKS + 1,)), dma((CHUNKS + 1,)),
            dma((2,)), dma((2,)), dma((1,)), dma((1,)), dma((1,)), dma((1,)),
            dma((2, 2, 2)), dma((2, 2, 2)),
            dma((7,)), dma((7,)), dma((15,)), dma((15,)),
        ],
        compiler_params=pltpu.CompilerParams(
            collective_id=0, has_side_effects=True, vmem_limit_bytes=48 * 2**20),
        cost_estimate=pl.CostEstimate(flops=20 * 10**9, bytes_accessed=16 * 2**20, transcendentals=10**6),
        name="conv_norm_silu",
    )(
        *(pltpu.with_memory_space_constraint(v, pltpu.HBM) for v in (
            latents, conv_weight.reshape(3, 3, 3 * C, C), conv_bias, norm_gain, norm_shift)))


def solution(mesh):
    spec = P("tm", "lat", "lon", None)
    return jax.shard_map(
        body, mesh=mesh, in_specs=(spec, P(), P(), P(), P()), out_specs=spec, check_vma=False)
```
